256 devices in a mesh: ctx: 32 (over x, z_hi, y), head: 8 (over z_lo, core).
Axes of the slice: x: 4, y: 4, z: 8 (z_hi: 2, z_lo: 4; z = z_hi * 4 + z_lo), core: 2. Of those that a mesh axis runs over, the one named last changes fastest.
Arguments:
- hidden: bfloat16 [8192, 8192], P('ctx', 'head'), may hold values from -9 to 9
- q_weight: bfloat16 [8192, 4096], P('ctx', 'head'), may hold values from -0.0625 to 0.0625
- regroup: int32 [4224], replicated, may hold values from 0 to 4223, each once
- student_rel: bfloat16 [8192, 768], P('ctx', 'head'), may hold values from -13 to 13
Outputs:
- student_grad: float32 [8192, 768], P('ctx', 'head')
- divergence: float32 [8192, 24], P('ctx', 'head')
The draws below stay inside these ranges and needn't reach their ends.
Inputs may be any that keep to these rules, and one draw needn't show every extreme that they name: `regroup`: a permutation of the relation channels; a value of 4096 or more means a channel of zeros.
All inputs are finite; a program needn't handle non-finite values.
Results may differ from the reference program's by a relative error of at most 0.0038.
Values may be sent and summed in bfloat16 or wider, within the bound.
No kernel may reach another device: no remote copies, remote signals or barrier semaphores. Data moves between devices by JAX's collectives and lax.ppermute only.
A program may use at most 128 MiB of HBM per device.

```python
import jax
import jax.numpy as jnp
from jax import lax

D = 8192
R = 24
DT = 176
DS = 32
BLOCK = 512
TQ = 4096
S = 8192


def far_twins(key, values):
    count = values.shape[0]
    reach = count // 4
    offset = jax.random.randint(key, (), 0, 2)
    index = jnp.arange(count, dtype=jnp.int32)
    chosen = ((index + offset) % 2 == 1) & (index // reach % 2 == 1)
    earlier = jnp.roll(values, reach, axis=0)
    return jnp.where(chosen[:, None], earlier, values)


def draw_hidden(key, part):
    key = jax.random.fold_in(key, 11)
    first, second = jax.random.split(key, 2)
    base = jnp.clip(jax.random.normal(first, (S, D), jnp.float32), -4.0, 4.0)
    return far_twins(second, base).astype(jnp.bfloat16)


def draw_student_rel(key, part):
    key = jax.random.fold_in(key, 23)
    base = jax.random.normal(key, (S, R * DS), jnp.float32)
    return jnp.clip(base, -4.0, 4.0).astype(jnp.bfloat16)


def levels(key, extent, cuts, low, high):
    def one(axis_at, shards_of):
        steps = jax.random.uniform(jax.random.fold_in(jax.random.fold_in(key, 6), axis_at), (shards_of,), jnp.float32, low / len(cuts), high / len(cuts))
        return jnp.repeat(jnp.exp(steps), extent[axis_at] // shards_of).reshape((-1,) + (1,) * (len(extent) - axis_at - 1))

    factor_of = one(*cuts[0])
    for cut in cuts[1:]:
        factor_of = factor_of * one(*cut)
    return factor_of


def gaussian(key, extent, scale, most, cuts=(), kind=jnp.bfloat16):
    entries = scale * jax.random.normal(key, extent, jnp.float32)
    if cuts:
        entries = entries * levels(key, extent, cuts, -0.22, 0.18)
    return jnp.clip(entries, -most, most).astype(kind)


def setup_inputs(seed: int = 0) -> dict:
    arg_keys = jax.random.split(jax.random.key(seed), 5)
    hidden = draw_hidden(jax.random.fold_in(arg_keys[4], 71), 0)
    q_weight = gaussian(arg_keys[1], (D, TQ), D ** -0.5, 0.0625, ((0, 32), (1, 8)))
    regroup = jax.random.permutation(arg_keys[2], R * DT).astype(jnp.int32)
    student_rel = draw_student_rel(jax.random.fold_in(arg_keys[4], 71), 0)
    return {"hidden": hidden, "q_weight": q_weight, "regroup": regroup, "student_rel": student_rel}


def head_terms(teacher_head, student_head):
    teacher_scale = 1.0 / (DT ** 0.5)
    student_scale = 1.0 / (DS ** 0.5)
    positions = jnp.arange(S, dtype=jnp.int32)

    def one_block(carry, block):
        start = block * BLOCK
        teacher_rows = lax.dynamic_slice_in_dim(teacher_head, start, BLOCK, 0)
        student_rows = lax.dynamic_slice_in_dim(student_head, start, BLOCK, 0)
        teacher_scores = jnp.dot(teacher_rows, teacher_head.T, preferred_element_type=jnp.float32) * teacher_scale
        student_scores = jnp.dot(student_rows, student_head.T, preferred_element_type=jnp.float32) * student_scale
        visible = positions[None, :] <= (start + jnp.arange(BLOCK, dtype=jnp.int32))[:, None]
        teacher_masked = jnp.where(visible, teacher_scores, -jnp.inf)
        student_masked = jnp.where(visible, student_scores, -jnp.inf)
        teacher_total = jax.nn.logsumexp(teacher_masked, axis=1)
        student_total = jax.nn.logsumexp(student_masked, axis=1)
        teacher_prob = jnp.exp(teacher_masked - teacher_total[:, None])
        student_prob = jnp.exp(student_masked - student_total[:, None])
        spread = jnp.where(visible, teacher_scores - student_scores, 0.0)
        divergence = jnp.sum(teacher_prob * spread, axis=1) - teacher_total + student_total
        weights = ((student_prob - teacher_prob) * student_scale).astype(jnp.bfloat16)
        query_side = jnp.dot(weights, student_head, preferred_element_type=jnp.float32)
        key_side = jnp.dot(weights.T, student_rows, preferred_element_type=jnp.float32)
        return carry + key_side, (divergence, query_side)

    initial = jnp.zeros((S, DS), jnp.float32)
    key_total, (divergence, query_side) = lax.scan(one_block, initial, jnp.arange(S // BLOCK, dtype=jnp.int32))
    return divergence.reshape(S), key_total + query_side.reshape(S, DS)


def reference(hidden, q_weight, regroup, student_rel):
    teacher_query = jnp.dot(hidden, q_weight, preferred_element_type=jnp.float32).astype(jnp.bfloat16)
    padded = jnp.concatenate([teacher_query, jnp.zeros((S, R * DT - TQ), jnp.bfloat16)], axis=1)
    teacher_rel = jnp.take(padded, regroup, axis=1)
    teacher_heads = teacher_rel.reshape(S, R, DT).transpose(1, 0, 2)
    student_heads = student_rel.reshape(S, R, DS).transpose(1, 0, 2)
    divergence, gradient = lax.map(lambda pair: head_terms(pair[0], pair[1]), (teacher_heads, student_heads))
    return gradient.transpose(1, 0, 2).reshape(S, R * DS), divergence.T
```

```python
import jax
import jax.numpy as jnp
import numpy as np
from jax import lax
from jax.experimental import pallas as pl
from jax.experimental.pallas import tpu as pltpu
from jax.sharding import Mesh
from jax.sharding import PartitionSpec as P

R = 24
DT = 176
DS = 32
TQ = 4096
ROWS = 256
SLOTS = 7
UNITS = SLOTS * 4
TASKS = 64
LOG2E = 1.4426950408889634
LN2 = 0.6931471805599453
TEACHER_SCALE = 1.0 / DT**0.5
STUDENT_SCALE = 1.0 / DS**0.5
LOWEST = -3.0e38
VMEM = 48 * 1024 * 1024
CTX = ("x", "zh", "y")
HEAD = ("zl", "core")


def back(step):
    return [(src, (src - step) % 4) for src in range(4)]


def forth(step):
    return [(src, (src + step) % 4) for src in range(4)]


SWAP = [(0, 1), (1, 0)]


def to_slots(block):
    rows = [lax.ppermute(block, "y", back(step)) for step in (1, 2, 3)]
    columns = [lax.ppermute(block, "x", back(step)) for step in (1, 2, 3)]
    return [block] + rows + columns


def to_owners(slots):
    rows = [lax.ppermute(slots[step], "y", forth(step)) for step in (1, 2, 3)]
    columns = [lax.ppermute(slots[3 + step], "x", forth(step)) for step in (1, 2, 3)]
    return [slots[0]] + rows + columns


def slot_of(device, block):
    (x, y), (bx, by) = device, block
    if bx == x:
        return (by - y) % 4
    return 3 + (bx - x) % 4


def holds(device, block):
    return device[0] == block[0] or device[1] == block[1]


def plan():
    places = [(x, y) for x in range(4) for y in range(4)]
    table = np.zeros((4, 2, 4, 2, TASKS), np.int32)
    counts = np.zeros((4, 2, 4), np.int32)

    def where(chunk):
        return (chunk // 8, chunk % 4), (chunk // 4) % 2

    for zh in range(2):
        load = {place: 0 for place in places}
        tiles = {place: [] for place in places}
        open_tiles = []
        for head in range(2):
            for query in range(32):
                if head == 1 and where(query)[1] != zh:
                    continue
                for key in range(query):
                    spots = [d for d in places if holds(d, where(query)[0]) and holds(d, where(key)[0])]
                    open_tiles.append((len(spots), head, query, key, spots))
        open_tiles.sort(key=lambda tile: tile[:4])
        for _, head, query, key, spots in open_tiles:
            best = min(spots, key=lambda d: (load[d], d))
            load[best] += 1
            tiles[best].append((head, query, key))
        for place in places:
            x, y = place

            def unit(head, chunk):
                block, half = where(chunk)
                return (slot_of(place, block) * 2 + (0 if half == zh else 1)) * 2 + head

            pairs = [(0, 0), (2, 2), (1, 1)]
            pairs += [(unit(h, q), unit(h, k)) for h, q, k in tiles[place]]
            counts[x, zh, y] = len(pairs)
            for index, (q, k) in enumerate(pairs):
                table[x, zh, y, 0, index] = q
                table[x, zh, y, 1, index] = k
    flat = np.concatenate([counts.reshape(32, 1), np.zeros((32, 127), np.int32)], axis=1)
    return np.concatenate([flat, table.reshape(32, 2 * TASKS)], axis=1)


def project_kernel(order, hidden, *refs):
    weights, out = refs[:8], refs[8]
    for block in range(4):
        total = None
        for piece in range(8):
            part = lax.dot_general(
                weights[piece][...],
                hidden[order[piece], block * ROWS : (block + 1) * ROWS, :],
                (((1,), (1,)), ((), ())),
                preferred_element_type=jnp.float32,
            )
            total = part if total is None else total + part
        out[block] = total


def project(order, hidden, weights):
    return pl.pallas_call(
        project_kernel,
        out_shape=jax.ShapeDtypeStruct((4, 3 * DT, ROWS), jnp.float32),
        in_specs=[pl.BlockSpec(memory_space=pltpu.SMEM)] + [pl.BlockSpec(memory_space=pltpu.VMEM)] * 9,
        out_specs=pl.BlockSpec(memory_space=pltpu.VMEM),
        compiler_params=pltpu.CompilerParams(vmem_limit_bytes=VMEM),
        name="project",
    )(order, hidden, *weights)


def fill_units(teacher, student, tch, tok, sch, sok):
    for slot in range(SLOTS):
        for sub in range(2):
            for head in range(2):
                unit = (slot * 2 + sub) * 2 + head
                tch[unit, :DT, :] = teacher[slot][sub, head * DT : (head + 1) * DT, :]
                tch[unit, DT:, :] = jnp.zeros((256 - DT, ROWS), jnp.bfloat16)
                sch[unit, :DS, :] = student[slot][sub, head * DS : (head + 1) * DS, :]
                sch[unit, DS:, :] = jnp.zeros((128 - DS, ROWS), jnp.bfloat16)

    def turn(unit, carry):
        tok[unit] = tch[unit].T
        sok[unit] = sch[unit].T
        return carry

    lax.fori_loop(0, UNITS, turn, 0)


def tile_scores(tch, tok, sch, sok, query, key, diagonal):
    teacher = jnp.dot(tok[key], tch[query], preferred_element_type=jnp.float32) * (TEACHER_SCALE * LOG2E)
    student = jnp.dot(sok[key], sch[query], preferred_element_type=jnp.float32) * (STUDENT_SCALE * LOG2E)
    if diagonal:
        keys = lax.broadcasted_iota(jnp.int32, (ROWS, ROWS), 0)
        queries = lax.broadcasted_iota(jnp.int32, (ROWS, ROWS), 1)
        visible = keys <= queries
        teacher = jnp.where(visible, teacher, LOWEST)
        student = jnp.where(visible, student, LOWEST)
    return teacher, student


def stats_kernel(tasks, *refs):
    teacher, student = refs[:SLOTS], refs[SLOTS : 2 * SLOTS]
    outs = refs[2 * SLOTS : 3 * SLOTS]
    tch, tok, sch, sok, stats = refs[3 * SLOTS :]
    fill_units(teacher, student, tch, tok, sch, sok)
    for unit in range(UNITS):
        stats[unit, 0:2, :] = jnp.full((2, ROWS), LOWEST, jnp.float32)
        stats[unit, 2:8, :] = jnp.zeros((6, ROWS), jnp.float32)

    def tile(task, diagonal):
        query = tasks[128 + task]
        key = tasks[128 + TASKS + task]
        t, s = tile_scores(tch, tok, sch, sok, query, key, diagonal)
        t_old = stats[query, 0:1, :]
        s_old = stats[query, 1:2, :]
        t_peak = jnp.maximum(jnp.max(t, axis=0, keepdims=True), t_old)
        s_peak = jnp.maximum(jnp.max(s, axis=0, keepdims=True), s_old)
        t_terms = jnp.exp2(t - t_peak)
        s_terms = jnp.exp2(s - s_peak)
        t_decay = jnp.exp2(t_old - t_peak)
        s_decay = jnp.exp2(s_old - s_peak)
        stats[query, 0:1, :] = t_peak
        stats[query, 1:2, :] = s_peak
        stats[query, 2:3, :] = stats[query, 2:3, :] * t_decay + jnp.sum(t_terms, axis=0, keepdims=True)
        stats[query, 3:4, :] = stats[query, 3:4, :] * s_decay + jnp.sum(s_terms, axis=0, keepdims=True)
        stats[query, 4:5, :] = stats[query, 4:5, :] * t_decay + jnp.sum(t_terms * (t - s), axis=0, keepdims=True)

    for task in range(3):
        tile(task, True)

    def one(task, carry):
        tile(task, False)
        return carry

    lax.fori_loop(3, tasks[0], one, 0)
    for slot in range(SLOTS):
        outs[slot][0:8, :] = stats[slot * 4]
        outs[slot][8:16, :] = stats[slot * 4 + 2]
        outs[slot][16:24, :] = stats[slot * 4 + 1]


UNIT_SCRATCH = [
    ((UNITS, 256, ROWS), jnp.bfloat16),
    ((UNITS, ROWS, 256), jnp.bfloat16),
    ((UNITS, 128, ROWS), jnp.bfloat16),
    ((UNITS, ROWS, 128), jnp.bfloat16),
]


def row_stats(tasks, teacher, student):
    return pl.pallas_call(
        stats_kernel,
        out_shape=[jax.ShapeDtypeStruct((24, ROWS), jnp.float32)] * SLOTS,
        in_specs=[pl.BlockSpec(memory_space=pltpu.SMEM)] + [pl.BlockSpec(memory_space=pltpu.VMEM)] * (2 * SLOTS),
        out_specs=[pl.BlockSpec(memory_space=pltpu.VMEM)] * SLOTS,
        scratch_shapes=[pltpu.VMEM(s, d) for s, d in UNIT_SCRATCH] + [pltpu.VMEM((UNITS, 8, ROWS), jnp.float32)],
        compiler_params=pltpu.CompilerParams(vmem_limit_bytes=VMEM),
        name="row_stats",
    )(tasks, *teacher, *student)


def merge_kernel(*refs):
    parts, totals, divergence = refs[:SLOTS], refs[SLOTS], refs[SLOTS + 1]
    totals[...] = jnp.zeros((8, ROWS), jnp.float32)
    divergence[...] = jnp.zeros((8, ROWS), jnp.float32)
    for unit in range(3):
        base = unit * 8
        rows = [[part[base + row : base + row + 1, :] for part in parts] for row in range(5)]
        t_peak, s_peak = rows[0][0], rows[1][0]
        for slot in range(1, SLOTS):
            t_peak = jnp.maximum(t_peak, rows[0][slot])
            s_peak = jnp.maximum(s_peak, rows[1][slot])
        t_mass = s_mass = weighted = jnp.zeros((1, ROWS), jnp.float32)
        for slot in range(SLOTS):
            t_decay = jnp.exp2(rows[0][slot] - t_peak)
            s_decay = jnp.exp2(rows[1][slot] - s_peak)
            t_mass = t_mass + rows[2][slot] * t_decay
            s_mass = s_mass + rows[3][slot] * s_decay
            weighted = weighted + rows[4][slot] * t_decay
        t_total = t_peak + jnp.log(t_mass) * LOG2E
        s_total = s_peak + jnp.log(s_mass) * LOG2E
        totals[unit : unit + 1, :] = t_total
        totals[4 + unit : 5 + unit, :] = s_total
        divergence[unit : unit + 1, :] = (weighted / t_mass - t_total + s_total) * LN2


def merge(parts):
    return pl.pallas_call(
        merge_kernel,
        out_shape=[jax.ShapeDtypeStruct((8, ROWS), jnp.float32)] * 2,
        in_specs=[pl.BlockSpec(memory_space=pltpu.VMEM)] * SLOTS,
        out_specs=[pl.BlockSpec(memory_space=pltpu.VMEM)] * 2,
        name="merge",
    )(*parts)


def grad_kernel(tasks, *refs):
    teacher, student, totals = refs[:SLOTS], refs[SLOTS : 2 * SLOTS], refs[2 * SLOTS : 3 * SLOTS]
    outs = refs[3 * SLOTS : 4 * SLOTS]
    tch, tok, sch, sok, total, grad = refs[4 * SLOTS :]
    fill_units(teacher, student, tch, tok, sch, sok)
    for slot in range(SLOTS):
        for row, unit in ((0, 0), (1, 2), (2, 1)):
            total[slot * 4 + unit, 0:1, :] = totals[slot][row : row + 1, :]
            total[slot * 4 + unit, 1:2, :] = totals[slot][4 + row : 5 + row, :]
    grad[...] = jnp.zeros((UNITS, DS, ROWS), jnp.float32)

    def tile(task, diagonal):
        query = tasks[128 + task]
        key = tasks[128 + TASKS + task]
        t, s = tile_scores(tch, tok, sch, sok, query, key, diagonal)
        t_prob = jnp.exp2(t - total[query, 0:1, :])
        s_prob = jnp.exp2(s - total[query, 1:2, :])
        weights = ((s_prob - t_prob) * STUDENT_SCALE).astype(jnp.bfloat16)
        grad[query] += jnp.dot(sch[key, :DS, :], weights, preferred_element_type=jnp.float32)
        grad[key] += lax.dot_general(
            sch[query, :DS, :], weights, (((1,), (1,)), ((), ())), preferred_element_type=jnp.float32
        )

    for task in range(3):
        tile(task, True)

    def one(task, carry):
        tile(task, False)
        return carry

    lax.fori_loop(3, tasks[0], one, 0)
    for slot in range(SLOTS):
        for unit in range(4):
            outs[slot][unit * DS : (unit + 1) * DS, :] = grad[slot * 4 + unit]


def gradients(tasks, teacher, student, totals):
    return pl.pallas_call(
        grad_kernel,
        out_shape=[jax.ShapeDtypeStruct((4 * DS, ROWS), jnp.float32)] * SLOTS,
        in_specs=[pl.BlockSpec(memory_space=pltpu.SMEM)] + [pl.BlockSpec(memory_space=pltpu.VMEM)] * (3 * SLOTS),
        out_specs=[pl.BlockSpec(memory_space=pltpu.VMEM)] * SLOTS,
        scratch_shapes=[pltpu.VMEM(s, d) for s, d in UNIT_SCRATCH]
        + [pltpu.VMEM((UNITS, 8, ROWS), jnp.float32), pltpu.VMEM((UNITS, DS, ROWS), jnp.float32)],
        compiler_params=pltpu.CompilerParams(vmem_limit_bytes=VMEM),
        name="gradients",
    )(tasks, *teacher, *student, *totals)


def pair_blocks(array, width, zh):
    heads = array.reshape(3, width, ROWS)
    mine = jnp.concatenate([jnp.where(zh == 0, heads[0], heads[1]), heads[2]], axis=0)
    theirs = jnp.concatenate([jnp.where(zh == 0, heads[1], heads[0]), heads[2]], axis=0)
    return jnp.stack([mine, lax.ppermute(theirs, "zh", SWAP)])


def shards(hidden, q_weight, regroup, student_rel):
    x, zh, y = lax.axis_index("x"), lax.axis_index("zh"), lax.axis_index("y")
    head = lax.axis_index(HEAD)
    place = x * 8 + zh * 4 + y
    tasks = lax.dynamic_index_in_dim(jnp.asarray(plan()), place, 0, keepdims=False)

    columns = lax.all_gather(q_weight.T, HEAD, axis=0, tiled=True)
    channels = lax.dynamic_slice_in_dim(regroup, head * (3 * DT), 3 * DT, 0)
    chosen = jnp.take(columns, jnp.minimum(channels, TQ - 1), axis=0)
    chosen = jnp.where((channels < TQ)[:, None], chosen, jnp.zeros((), jnp.bfloat16))

    quarter = lax.all_to_all(hidden.reshape(ROWS, 4, ROWS).transpose(1, 0, 2), "y", 0, 0)
    features = lax.all_gather(quarter.reshape(4 * ROWS, ROWS), HEAD, axis=0)

    other = lax.ppermute(chosen, "zh", SWAP)
    pieces = [chosen] + [lax.ppermute(chosen, "x", back(step)) for step in (1, 2, 3)]
    pieces += [other] + [lax.ppermute(other, "x", back(step)) for step in (1, 2, 3)]
    around = (x + jnp.arange(4, dtype=jnp.int32)) % 4 * 2
    order = jnp.concatenate([around + zh, around + 1 - zh])

    student = to_slots(pair_blocks(student_rel.T, DS, zh))

    partial_query = project(order, features, pieces)
    own_query = jnp.sum(lax.all_to_all(partial_query, "y", 0, 0), axis=0).astype(jnp.bfloat16)
    teacher = to_slots(pair_blocks(own_query, DT, zh))

    parts = to_owners(row_stats(tasks, teacher, student))
    totals, divergence = merge(parts)
    grads = to_owners(gradients(tasks, teacher, student, to_slots(totals)))
    grad = grads[0]
    for piece in grads[1:]:
        grad = grad + piece

    swapped = lax.ppermute(grad[2 * DS :], "zh", SWAP)
    first = jnp.where(zh == 0, grad[:DS], swapped[:DS])
    second = jnp.where(zh == 0, swapped[:DS], grad[:DS])
    third = grad[DS : 2 * DS] + swapped[DS:]
    student_grad = jnp.concatenate([first, second, third], axis=0).T

    away = lax.ppermute(divergence[1:2], "zh", SWAP)[0]
    first = jnp.where(zh == 0, divergence[0], away)
    second = jnp.where(zh == 0, away, divergence[0])
    return student_grad, jnp.stack([first, second, divergence[2]], axis=1)


def solution(mesh):
    whole = Mesh(mesh.devices.reshape(4, 2, 4, 4, 2), CTX + HEAD)
    split = P(CTX, HEAD)
    return jax.shard_map(
        shards,
        mesh=whole,
        in_specs=(split, split, P(), split),
        out_specs=(split, split),
        check_vma=False,
    )
```

```python
import jax
import jax.numpy as jnp
import numpy as np
from jax import lax
from jax.experimental import pallas as pl
from jax.experimental.pallas import tpu as pltpu
from jax.sharding import Mesh
from jax.sharding import PartitionSpec as P

R = 24
DT = 176
DS = 32
TQ = 4096
ROWS = 256
SLOTS = 7
UNITS = SLOTS * 4
NO_UNIT = UNITS
LOG2E = 1.4426950408889634
LN2 = 0.6931471805599453
TEACHER_SCALE = 1.0 / DT**0.5
STUDENT_SCALE = 1.0 / DS**0.5
LOWEST = -3.0e38
VMEM = 48 * 1024 * 1024
CTX = ("x", "zh", "y")
HEAD = ("zl", "core")


def back(step):
    return [(src, (src - step) % 4) for src in range(4)]


def forth(step):
    return [(src, (src + step) % 4) for src in range(4)]


SWAP = [(0, 1), (1, 0)]


def to_slots(block):
    rows = [lax.ppermute(block, "y", back(step)) for step in (1, 2, 3)]
    columns = [lax.ppermute(block, "x", back(step)) for step in (1, 2, 3)]
    return [block] + rows + columns


def to_owners(slots):
    rows = [lax.ppermute(slots[step], "y", forth(step)) for step in (1, 2, 3)]
    columns = [lax.ppermute(slots[3 + step], "x", forth(step)) for step in (1, 2, 3)]
    return [slots[0]] + rows + columns


def slot_of(device, block):
    (x, y), (bx, by) = device, block
    if bx == x:
        return (by - y) % 4
    return 3 + (bx - x) % 4


def holds(device, block):
    return device[0] == block[0] or device[1] == block[1]


def by_row(x, y, sub, head):
    return sub == 0 if head == 0 else (x + y) % 2 == 0


def plan():
    places = [(x, y) for x in range(4) for y in range(4)]
    table = np.zeros((4, 2, 4, 256), np.int32)

    def where(chunk):
        return (chunk // 8, chunk % 4), (chunk // 4) % 2

    for zh in range(2):
        load = {place: 0 for place in places}
        keys_of = {place: {} for place in places}
        open_tiles = []
        for head in range(2):
            for query in range(32):
                block, half = where(query)
                sub = 0 if half == zh else 1
                if head == 1 and sub == 1:
                    continue
                line = 0 if by_row(*block, sub, head) else 1
                for key in range(query):
                    spots = [
                        d for d in places if d[line] == block[line] and holds(d, block) and holds(d, where(key)[0])
                    ]
                    open_tiles.append((len(spots), head, query, key, spots))
        open_tiles.sort(key=lambda tile: tile[:4])
        for _, head, query, key, spots in open_tiles:
            odd = {d: len(keys_of[d].get((head, query), ())) % 2 for d in spots}
            best = min(spots, key=lambda d: (load[d] - odd[d], d))
            load[best] += 1
            keys_of[best].setdefault((head, query), []).append(key)
        for place in places:
            x, y = place

            def unit(head, chunk):
                block, half = where(chunk)
                return (slot_of(place, block) * 2 + (0 if half == zh else 1)) * 2 + head

            tasks = []
            for (head, query), keys in sorted(keys_of[place].items()):
                units = [unit(head, key) for key in sorted(keys)]
                if len(units) % 2:
                    units.append(NO_UNIT)
                tasks += [(unit(head, query), a, b) for a, b in zip(units[::2], units[1::2])]
            if len(tasks) % 2:
                tasks.append((NO_UNIT, NO_UNIT, NO_UNIT))
            row = table[x, zh, y]
            row[0] = len(tasks) // 2
            for index, task in enumerate(tasks):
                row[1 + 3 * index : 4 + 3 * index] = task
    return table.reshape(32, 256)


def stack_kernel(*refs):
    out = refs[-1]
    for index in range(4):
        out[index * ROWS : (index + 1) * ROWS, :] = refs[index][...]


def stack(blocks, after):
    return pl.pallas_call(
        stack_kernel,
        out_shape=jax.ShapeDtypeStruct((4 * ROWS, ROWS), jnp.bfloat16),
        in_specs=[pl.BlockSpec(memory_space=pltpu.VMEM)] * 4 + [pl.BlockSpec(memory_space=pl.ANY)] * len(after),
        out_specs=pl.BlockSpec(memory_space=pltpu.VMEM),
        cost_estimate=pl.CostEstimate(flops=0, bytes_accessed=1 << 20, transcendentals=0),
        name="stack",
    )(*blocks, *after)


def hold_kernel(value, after, out):
    out[...] = value[...]


def hold(value, after):
    return pl.pallas_call(
        hold_kernel,
        out_shape=jax.ShapeDtypeStruct(value.shape, value.dtype),
        in_specs=[pl.BlockSpec(memory_space=pltpu.VMEM), pl.BlockSpec(memory_space=pl.ANY)],
        out_specs=pl.BlockSpec(memory_space=pltpu.VMEM),
        name="hold",
    )(value, after)


def choose_kernel(bases, channels, *refs):
    pieces, out = refs[:8], refs[-1]
    for head in range(3):
        rows = slice(head * DT, (head + 1) * DT)
        total = None
        for index, piece in enumerate(pieces):
            places = lax.broadcasted_iota(jnp.int32, (DT, piece.shape[0]), 1)
            picked = jnp.where(channels[rows, :] - bases[index] == places, 1.0, 0.0).astype(jnp.bfloat16)
            part = jnp.dot(picked, piece[...], preferred_element_type=jnp.float32)
            total = part if total is None else total + part
        out[rows, :] = total.astype(jnp.bfloat16)


def choose(bases, channels, pieces, after):
    size = channels.shape[0]
    return pl.pallas_call(
        choose_kernel,
        out_shape=jax.ShapeDtypeStruct((size, ROWS), jnp.bfloat16),
        in_specs=[pl.BlockSpec(memory_space=pltpu.SMEM)]
        + [pl.BlockSpec(memory_space=pltpu.VMEM)] * 9
        + [pl.BlockSpec(memory_space=pl.ANY)] * len(after),
        out_specs=pl.BlockSpec(memory_space=pltpu.VMEM),
        compiler_params=pltpu.CompilerParams(vmem_limit_bytes=VMEM),
        cost_estimate=pl.CostEstimate(flops=2 * size * ROWS * TQ, bytes_accessed=3 << 20, transcendentals=0),
        name="choose",
    )(bases, channels, *pieces, *after)


def project_kernel(order, hidden, *refs):
    weights, outs, (wide, tall) = refs[:8], refs[-6:-2], refs[-2:]
    for piece in range(8):
        wide[:, piece * ROWS : (piece + 1) * ROWS] = weights[piece][...]
    for block in (2, 1, 3, 0):
        for piece in range(8):
            tall[:, piece * ROWS : (piece + 1) * ROWS] = hidden[order[piece], block * ROWS : (block + 1) * ROWS, :]
        outs[block][...] = lax.dot_general(
            wide[...], tall[...], (((1,), (1,)), ((), ())), preferred_element_type=jnp.float32
        )


def project(order, hidden, weights):
    size = weights[0].shape[0]
    return pl.pallas_call(
        project_kernel,
        out_shape=[jax.ShapeDtypeStruct((size, ROWS), jnp.float32)] * 4,
        in_specs=[pl.BlockSpec(memory_space=pltpu.SMEM)]
        + [pl.BlockSpec(memory_space=pltpu.VMEM)] * 9,
        out_specs=[pl.BlockSpec(memory_space=pltpu.VMEM)] * 4,
        scratch_shapes=[pltpu.VMEM((size, 8 * ROWS), jnp.bfloat16), pltpu.VMEM((ROWS, 8 * ROWS), jnp.bfloat16)],
        compiler_params=pltpu.CompilerParams(vmem_limit_bytes=VMEM),
        cost_estimate=pl.CostEstimate(
            flops=2 * 4 * size * ROWS * 8 * ROWS, bytes_accessed=(8 << 20) + 16 * size * ROWS, transcendentals=0
        ),
        name="project",
    )(order, hidden, *weights)


def finish_kernel(zh, first, second, third, fourth, *refs):
    mine, theirs = refs[-2:]
    for head in range(3):
        rows = slice(head * DT, (head + 1) * DT)
        total = ((first[rows, :] + second[rows, :]) + (third[rows, :] + fourth[rows, :])).astype(jnp.bfloat16)
        if head == 2:
            mine[DT:, :] = total
            theirs[DT:, :] = total
        else:

            @pl.when(zh[0] == head)
            def _():
                mine[:DT, :] = total

            @pl.when(zh[0] != head)
            def _():
                theirs[:DT, :] = total


def finish(zh, parts, after):
    return pl.pallas_call(
        finish_kernel,
        out_shape=[jax.ShapeDtypeStruct((2 * DT, ROWS), jnp.bfloat16)] * 2,
        in_specs=[pl.BlockSpec(memory_space=pltpu.SMEM)] + [pl.BlockSpec(memory_space=pltpu.VMEM)] * 4
        + [pl.BlockSpec(memory_space=pl.ANY)] * len(after),
        out_specs=[pl.BlockSpec(memory_space=pltpu.VMEM)] * 2,
        compiler_params=pltpu.CompilerParams(vmem_limit_bytes=VMEM),
        name="finish",
    )(zh.reshape(1), *parts, *after)


def fill_units(teacher, student, units):
    tch, tok, sch, sok = units
    zero = jnp.zeros((), jnp.bfloat16)
    t_pad = jnp.where(lax.broadcasted_iota(jnp.int32, (256 - DT, ROWS), 0) == 0, 1.0, 0.0).astype(jnp.bfloat16)
    s_pad = jnp.where(lax.broadcasted_iota(jnp.int32, (128 - DS, ROWS), 0) == 0, 1.0, 0.0).astype(jnp.bfloat16)
    for slot in range(SLOTS):
        for sub in range(2):
            for head in range(2):
                unit = (slot * 2 + sub) * 2 + head
                t = teacher[sub * SLOTS + slot][head * DT : (head + 1) * DT, :]
                s = student[slot][sub, head * DS : (head + 1) * DS, :]
                tch[unit, :DT, :] = t
                tch[unit, DT:, :] = t_pad
                sch[unit, :DS, :] = s
                sch[unit, DS:, :] = s_pad
                tok[unit] = jnp.concatenate([t, jnp.zeros((256 - DT, ROWS), jnp.bfloat16)], axis=0).T
                sok[unit] = jnp.concatenate([s, jnp.zeros((128 - DS, ROWS), jnp.bfloat16)], axis=0).T
    tch[NO_UNIT] = jnp.full((256, ROWS), zero)
    sch[NO_UNIT] = jnp.full((128, ROWS), zero)
    t_column = lax.broadcasted_iota(jnp.int32, (ROWS, 256), 1) == DT
    s_column = lax.broadcasted_iota(jnp.int32, (ROWS, 128), 1) == DS
    tok[NO_UNIT] = jnp.where(t_column, LOWEST, 0.0).astype(jnp.bfloat16)
    sok[NO_UNIT] = jnp.where(s_column, LOWEST, 0.0).astype(jnp.bfloat16)


def score(units, query, key):
    tch, tok, sch, sok = units
    return (
        jnp.dot(tok[key], tch[query], preferred_element_type=jnp.float32),
        jnp.dot(sok[key], sch[query], preferred_element_type=jnp.float32),
    )


def diagonal_scores(units, unit):
    t, s = score(units, unit, unit)
    visible = lax.broadcasted_iota(jnp.int32, (ROWS, ROWS), 0) <= lax.broadcasted_iota(jnp.int32, (ROWS, ROWS), 1)
    return jnp.where(visible, t, LOWEST), jnp.where(visible, s, LOWEST)


def walk(tasks, units, buffers, use):
    pairs = tasks[0]

    def load(task, buffer):
        query = tasks[1 + 3 * task]
        for half in range(2):
            t, s = score(units, query, tasks[2 + half + 3 * task])
            buffer[0, half * ROWS : (half + 1) * ROWS, :] = t
            buffer[1, half * ROWS : (half + 1) * ROWS, :] = s

    def take(task, buffer):
        use(tasks[1 + 3 * task], (tasks[2 + 3 * task], tasks[3 + 3 * task]), buffer)

    load(0, buffers[0])

    def two(pair, carry):
        load(2 * pair + 1, buffers[1])
        take(2 * pair, buffers[0])
        load(jnp.minimum(2 * pair + 2, 2 * pairs - 1), buffers[0])
        take(2 * pair + 1, buffers[1])
        return carry

    lax.fori_loop(0, pairs, two, 0)


def add_scores(stats, query, t, s):
    t = t * (TEACHER_SCALE * LOG2E)
    s = s * (STUDENT_SCALE * LOG2E)
    old = stats[query]
    t_peak = jnp.maximum(jnp.max(t, axis=0, keepdims=True), old[0:1])
    s_peak = jnp.maximum(jnp.max(s, axis=0, keepdims=True), old[1:2])
    t_terms = jnp.exp2(t - t_peak)
    s_terms = jnp.exp2(s - s_peak)
    t_decay = jnp.exp2(old[0:1] - t_peak)
    s_decay = jnp.exp2(old[1:2] - s_peak)
    stats[query, 0:1, :] = t_peak
    stats[query, 1:2, :] = s_peak
    stats[query, 2:3, :] = old[2:3] * t_decay + jnp.sum(t_terms, axis=0, keepdims=True)
    stats[query, 3:4, :] = old[3:4] * s_decay + jnp.sum(s_terms, axis=0, keepdims=True)
    stats[query, 4:5, :] = old[4:5] * t_decay + jnp.sum(t_terms * (t - s), axis=0, keepdims=True)


DIAGONAL = (0, 2, 1)
ROW_UNITS = (0, 1)
COLUMN_UNITS = (2, 1)


def stats_kernel(tasks, *refs):
    teacher, student = refs[: 2 * SLOTS], refs[2 * SLOTS : 3 * SLOTS]
    along_row, along_column = refs[3 * SLOTS : 3 * SLOTS + 2]
    rest = refs[3 * SLOTS + 2 :]
    units, stats, buffers = rest[:4], rest[4], rest[5:]
    fill_units(teacher, student, units)
    for unit in range(UNITS + 1):
        stats[unit, 0:2, :] = jnp.full((2, ROWS), LOWEST, jnp.float32)
        stats[unit, 2:8, :] = jnp.zeros((6, ROWS), jnp.float32)
    for unit in DIAGONAL:
        add_scores(stats, unit, *diagonal_scores(units, unit))
    walk(tasks, units, buffers, lambda query, keys, buffer: add_scores(stats, query, buffer[0], buffer[1]))
    for step in range(4):
        for out, slot, chosen in (
            (along_row, step, ROW_UNITS),
            (along_column, 3 + step if step else 0, COLUMN_UNITS),
        ):
            for place, unit in enumerate(chosen):
                first = (step * 2 + place) * 8
                out[first : first + 8, :] = stats[slot * 4 + unit]


UNIT_SCRATCH = [
    ((UNITS + 1, 256, ROWS), jnp.bfloat16),
    ((UNITS + 1, ROWS, 256), jnp.bfloat16),
    ((UNITS + 1, 128, ROWS), jnp.bfloat16),
    ((UNITS + 1, ROWS, 128), jnp.bfloat16),
]
BUFFERS = [((2, 2 * ROWS, ROWS), jnp.float32)] * 2


def row_stats(tasks, teacher, student):
    scratch = UNIT_SCRATCH + [((UNITS + 1, 8, ROWS), jnp.float32)] + BUFFERS
    return pl.pallas_call(
        stats_kernel,
        out_shape=[jax.ShapeDtypeStruct((64, ROWS), jnp.float32)] * 2,
        in_specs=[pl.BlockSpec(memory_space=pltpu.SMEM)] + [pl.BlockSpec(memory_space=pltpu.VMEM)] * (3 * SLOTS),
        out_specs=[pl.BlockSpec(memory_space=pltpu.VMEM)] * 2,
        scratch_shapes=[pltpu.VMEM(s, d) for s, d in scratch],
        compiler_params=pltpu.CompilerParams(vmem_limit_bytes=VMEM),
        name="row_stats",
    )(tasks, *teacher, *student)


def merge_rows(parts):
    t_peak, s_peak = parts[0][0:1], parts[0][1:2]
    for part in parts[1:]:
        t_peak = jnp.maximum(t_peak, part[0:1])
        s_peak = jnp.maximum(s_peak, part[1:2])
    t_mass = s_mass = weighted = jnp.zeros((1, ROWS), jnp.float32)
    for part in parts:
        t_decay = jnp.exp2(part[0:1] - t_peak)
        t_mass = t_mass + part[2:3] * t_decay
        s_mass = s_mass + part[3:4] * jnp.exp2(part[1:2] - s_peak)
        weighted = weighted + part[4:5] * t_decay
    t_total = t_peak + jnp.log(t_mass) * LOG2E
    s_total = s_peak + jnp.log(s_mass) * LOG2E
    return t_total, s_total, (weighted / t_mass - t_total + s_total) * LN2


def merge_parts(rows, columns, total, divergence):
    def of(line, step, place):
        entries = [((step - ahead) % 4 * 2 + place) * 8 for ahead in range(4)]
        return [part[entry : entry + 8, :] for part, entry in zip(line, entries)]

    divergence[...] = jnp.zeros((8, ROWS), jnp.float32)
    cases = [(0, 0, of(rows, 0, 0)), (0, 2, of(columns, 0, 0)), (0, 1, of(rows, 0, 1) + of(columns, 0, 1)[1:])]
    for step in (1, 2, 3):
        cases += [(step, unit, of(rows, step, place)) for place, unit in enumerate(ROW_UNITS)]
        cases += [(3 + step, unit, of(columns, step, place)) for place, unit in enumerate(COLUMN_UNITS)]
    for index, (slot, unit, parts) in enumerate(cases):
        t_total, s_total, value = merge_rows(parts)
        total[slot * 4 + unit, 0:1, :] = t_total
        total[slot * 4 + unit, 1:2, :] = s_total
        if index < 3:
            divergence[index : index + 1, :] = value


def grad_kernel(tasks, *refs):
    teacher, student = refs[: 2 * SLOTS], refs[2 * SLOTS : 3 * SLOTS]
    rows, columns = refs[3 * SLOTS : 3 * SLOTS + 4], refs[3 * SLOTS + 4 : 3 * SLOTS + 8]
    outs, divergence = refs[3 * SLOTS + 8 : 4 * SLOTS + 8], refs[4 * SLOTS + 8]
    rest = refs[4 * SLOTS + 9 :]
    units, total, grad, buffers = rest[:4], rest[4], rest[5], rest[6:]
    fill_units(teacher, student, units)
    sch = units[2]
    merge_parts(rows, columns, total, divergence)
    total[NO_UNIT] = jnp.full((8, ROWS), -LOWEST, jnp.float32)
    grad[...] = jnp.zeros((UNITS + 1, DS, ROWS), jnp.float32)

    def add(query, key, t, s):
        t_prob = jnp.exp2(t * (TEACHER_SCALE * LOG2E) - total[query, 0:1, :])
        s_prob = jnp.exp2(s * (STUDENT_SCALE * LOG2E) - total[query, 1:2, :])
        weights = ((s_prob - t_prob) * STUDENT_SCALE).astype(jnp.bfloat16)
        grad[query] += jnp.dot(sch[key, :DS, :], weights, preferred_element_type=jnp.float32)
        grad[key] += lax.dot_general(
            sch[query, :DS, :], weights, (((1,), (1,)), ((), ())), preferred_element_type=jnp.float32
        )

    def use(query, keys, buffer):
        for half in range(2):
            part = slice(half * ROWS, (half + 1) * ROWS)
            add(query, keys[half], buffer[0, part, :], buffer[1, part, :])

    for unit in DIAGONAL:
        add(unit, unit, *diagonal_scores(units, unit))
    walk(tasks, units, buffers, use)
    for slot in range(SLOTS):
        for unit in range(4):
            outs[slot][unit * DS : (unit + 1) * DS, :] = grad[slot * 4 + unit]


def gradients(tasks, teacher, student, rows, columns):
    scratch = UNIT_SCRATCH + [((UNITS + 1, 8, ROWS), jnp.float32), ((UNITS + 1, DS, ROWS), jnp.float32)] + BUFFERS
    outs = pl.pallas_call(
        grad_kernel,
        out_shape=[jax.ShapeDtypeStruct((4 * DS, ROWS), jnp.float32)] * SLOTS
        + [jax.ShapeDtypeStruct((8, ROWS), jnp.float32)],
        in_specs=[pl.BlockSpec(memory_space=pltpu.SMEM)] + [pl.BlockSpec(memory_space=pltpu.VMEM)] * (3 * SLOTS + 8),
        out_specs=[pl.BlockSpec(memory_space=pltpu.VMEM)] * (SLOTS + 1),
        scratch_shapes=[pltpu.VMEM(s, d) for s, d in scratch],
        compiler_params=pltpu.CompilerParams(vmem_limit_bytes=VMEM),
        name="gradients",
    )(tasks, *teacher, *student, *rows, *columns)
    return outs[:SLOTS], outs[SLOTS]


def to_line(block, axis):
    return [block] + [lax.ppermute(block, axis, back(step)) for step in (1, 2, 3)]


def pair_students(student, zh):
    heads = student.reshape(3, DS, ROWS)
    mine = jnp.concatenate([jnp.where(zh == 0, heads[0], heads[1]), heads[2]], axis=0)
    theirs = jnp.concatenate([jnp.where(zh == 0, heads[1], heads[0]), heads[2]], axis=0)
    return jnp.stack([mine, lax.ppermute(theirs, "zh", SWAP)])


def shards(hidden, q_weight, regroup, student_rel):
    x, zh, y = lax.axis_index("x"), lax.axis_index("zh"), lax.axis_index("y")
    head = lax.axis_index(HEAD)
    place = x * 8 + zh * 4 + y
    tasks = lax.dynamic_index_in_dim(jnp.asarray(plan()), place, 0, keepdims=False)

    zl, core = lax.axis_index("zl"), lax.axis_index("core")
    line = to_line(q_weight.T, "zl")
    columns = line + [lax.ppermute(piece, "core", SWAP) for piece in line]
    owners = (zl + jnp.arange(4, dtype=jnp.int32)) % 4 * 2
    bases = jnp.concatenate([owners + core, owners + 1 - core]) * columns[0].shape[0]

    quarters = [lax.dynamic_slice(hidden, (0, (y + step) % 4 * ROWS), (ROWS, ROWS)) for step in range(4)]
    quarters = quarters[:1] + [lax.ppermute(quarters[step], "y", forth(step)) for step in (1, 2, 3)]
    features = lax.all_gather(stack(quarters, line[1:2]), HEAD, axis=0)

    channels = lax.dynamic_slice_in_dim(regroup, head * (3 * DT), 3 * DT, 0)
    chosen = choose(bases, channels[:, None], columns, ())
    pair = pair_students(student_rel.T, zh)
    other = lax.ppermute(chosen, "zh", SWAP)
    pieces = to_line(chosen, "x") + to_line(other, "x")
    around = (x + jnp.arange(4, dtype=jnp.int32)) % 4 * 2
    order = jnp.concatenate([around + zh, around + 1 - zh])

    student = to_slots(hold(pair, pieces[5]))

    parts = project(order, features, pieces)
    moved = [lax.ppermute(parts[step], "y", back(step)) for step in (1, 2, 3)]
    mine, theirs = finish(zh, [parts[0]] + moved, student)
    partners = lax.ppermute(theirs, "zh", SWAP)
    teacher = to_slots(mine) + to_slots(partners)

    along_row, along_column = row_stats(tasks, teacher, student)
    grads, divergence = gradients(tasks, teacher, student, to_line(along_row, "y"), to_line(along_column, "x"))
    grads = to_owners(grads)
    grad = grads[0]
    for piece in grads[1:]:
        grad = grad + piece

    swapped = lax.ppermute(grad[2 * DS :], "zh", SWAP)
    first = jnp.where(zh == 0, grad[:DS], swapped[:DS])
    second = jnp.where(zh == 0, swapped[:DS], grad[:DS])
    third = grad[DS : 2 * DS] + swapped[DS:]
    student_grad = jnp.concatenate([first, second, third], axis=0).T

    away = lax.ppermute(divergence[1:2], "zh", SWAP)[0]
    first = jnp.where(zh == 0, divergence[0], away)
    second = jnp.where(zh == 0, away, divergence[0])
    return student_grad, jnp.stack([first, second, divergence[2]], axis=1)


def solution(mesh):
    whole = Mesh(mesh.devices.reshape(4, 2, 4, 4, 2), CTX + HEAD)
    split = P(CTX, HEAD)
    return jax.shard_map(
        shards,
        mesh=whole,
        in_specs=(split, split, P(), split),
        out_specs=(split, split),
        check_vma=False,
    )
```

```python
import jax
import jax.numpy as jnp
import numpy as np
from jax import lax
from jax.experimental import pallas as pl
from jax.experimental.pallas import tpu as pltpu
from jax.sharding import Mesh
from jax.sharding import PartitionSpec as P

R = 24
DT = 176
DS = 32
TQ = 4096
ROWS = 256
SLOTS = 7
UNITS = SLOTS * 4
NO_UNIT = UNITS
LOG2E = 1.4426950408889634
LN2 = 0.6931471805599453
TEACHER_SCALE = 1.0 / DT**0.5
STUDENT_SCALE = 1.0 / DS**0.5
LOWEST = -3.0e38
VMEM = 48 * 1024 * 1024
CTX = ("x", "zh", "y")
HEAD = ("zl", "core")


def back(step):
    return [(src, (src - step) % 4) for src in range(4)]


def forth(step):
    return [(src, (src + step) % 4) for src in range(4)]


SWAP = [(0, 1), (1, 0)]


def to_slots(block):
    rows = [lax.ppermute(block, "y", back(step)) for step in (1, 2, 3)]
    columns = [lax.ppermute(block, "x", back(step)) for step in (1, 2, 3)]
    return [block] + rows + columns


def to_owners(slots):
    rows = [lax.ppermute(slots[step], "y", forth(step)) for step in (1, 2, 3)]
    columns = [lax.ppermute(slots[3 + step], "x", forth(step)) for step in (1, 2, 3)]
    return [slots[0]] + rows + columns


def slot_of(device, block):
    (x, y), (bx, by) = device, block
    if bx == x:
        return (by - y) % 4
    return 3 + (bx - x) % 4


def holds(device, block):
    return device[0] == block[0] or device[1] == block[1]


def by_row(x, y, sub, head):
    return sub == 0 if head == 0 else (x + y) % 2 == 0


def plan():
    places = [(x, y) for x in range(4) for y in range(4)]
    table = np.zeros((4, 2, 4, 256), np.int32)

    def where(chunk):
        return (chunk // 8, chunk % 4), (chunk // 4) % 2

    for zh in range(2):
        load = {place: 0 for place in places}
        keys_of = {place: {} for place in places}
        open_tiles = []
        for head in range(2):
            for query in range(32):
                block, half = where(query)
                sub = 0 if half == zh else 1
                if head == 1 and sub == 1:
                    continue
                line = 0 if by_row(*block, sub, head) else 1
                for key in range(query):
                    spots = [
                        d for d in places if d[line] == block[line] and holds(d, block) and holds(d, where(key)[0])
                    ]
                    open_tiles.append((len(spots), head, query, key, spots))
        open_tiles.sort(key=lambda tile: tile[:4])
        for _, head, query, key, spots in open_tiles:
            odd = {d: len(keys_of[d].get((head, query), ())) % 2 for d in spots}
            best = min(spots, key=lambda d: (load[d] - odd[d], d))
            load[best] += 1
            keys_of[best].setdefault((head, query), []).append(key)
        for place in places:
            x, y = place

            def unit(head, chunk):
                block, half = where(chunk)
                return (slot_of(place, block) * 2 + (0 if half == zh else 1)) * 2 + head

            tasks = []
            for (head, query), keys in sorted(keys_of[place].items()):
                units = [unit(head, key) for key in sorted(keys)]
                if len(units) % 2:
                    units.append(NO_UNIT)
                tasks += [(unit(head, query), a, b) for a, b in zip(units[::2], units[1::2])]
            if len(tasks) % 2:
                tasks.append((NO_UNIT, NO_UNIT, NO_UNIT))
            row = table[x, zh, y]
            row[0] = len(tasks) // 2
            for index, task in enumerate(tasks):
                row[1 + 3 * index : 4 + 3 * index] = task
    return table.reshape(32, 256)


def stack_kernel(*refs):
    out = refs[-1]
    for index in range(4):
        out[index * ROWS : (index + 1) * ROWS, :] = refs[index][...]


def stack(blocks, after):
    return pl.pallas_call(
        stack_kernel,
        out_shape=jax.ShapeDtypeStruct((4 * ROWS, ROWS), jnp.bfloat16),
        in_specs=[pl.BlockSpec(memory_space=pltpu.VMEM)] * 4 + [pl.BlockSpec(memory_space=pl.ANY)] * len(after),
        out_specs=pl.BlockSpec(memory_space=pltpu.VMEM),
        cost_estimate=pl.CostEstimate(flops=0, bytes_accessed=1 << 20, transcendentals=0),
        name="stack",
    )(*blocks, *after)


def choose_kernel(bases, channels, *refs):
    pieces, out = refs[:8], refs[-1]
    for head in range(3):
        rows = slice(head * DT, (head + 1) * DT)
        total = None
        for index, piece in enumerate(pieces):
            places = lax.broadcasted_iota(jnp.int32, (DT, piece.shape[0]), 1)
            picked = jnp.where(channels[rows, :] - bases[index] == places, 1.0, 0.0).astype(jnp.bfloat16)
            part = jnp.dot(picked, piece[...], preferred_element_type=jnp.float32)
            total = part if total is None else total + part
        out[rows, :] = total.astype(jnp.bfloat16)


def choose(bases, channels, pieces, after):
    size = channels.shape[0]
    return pl.pallas_call(
        choose_kernel,
        out_shape=jax.ShapeDtypeStruct((size, ROWS), jnp.bfloat16),
        in_specs=[pl.BlockSpec(memory_space=pltpu.SMEM)]
        + [pl.BlockSpec(memory_space=pltpu.VMEM)] * 9
        + [pl.BlockSpec(memory_space=pl.ANY)] * len(after),
        out_specs=pl.BlockSpec(memory_space=pltpu.VMEM),
        compiler_params=pltpu.CompilerParams(vmem_limit_bytes=VMEM),
        cost_estimate=pl.CostEstimate(flops=2 * size * ROWS * TQ, bytes_accessed=3 << 20, transcendentals=0),
        name="choose",
    )(bases, channels, *pieces, *after)


def project_kernel(order, hidden, *refs):
    weights, outs, (wide, tall) = refs[:8], refs[-10:-2], refs[-2:]
    zh = order[8]
    for piece in range(8):
        columns = slice(piece * ROWS, (piece + 1) * ROWS)
        for place, head in enumerate((1 - zh, 2, zh)):
            rows = pl.ds(pl.multiple_of(head * DT, 16), DT)
            wide[place * DT : (place + 1) * DT, columns] = weights[piece][rows, :]
    for block in (2, 1, 3, 0):
        for piece in range(8):
            tall[:, piece * ROWS : (piece + 1) * ROWS] = hidden[order[piece], block * ROWS : (block + 1) * ROWS, :]
        for out, rows in ((outs[block], slice(0, 2 * DT)), (outs[4 + block], slice(2 * DT, 3 * DT))):
            out[...] = lax.dot_general(
                wide[rows, :], tall[...], (((1,), (1,)), ((), ())), preferred_element_type=jnp.float32
            )


def project(order, hidden, weights):
    sizes = [2 * DT] * 4 + [DT] * 4
    outs = pl.pallas_call(
        project_kernel,
        out_shape=[jax.ShapeDtypeStruct((size, ROWS), jnp.float32) for size in sizes],
        in_specs=[pl.BlockSpec(memory_space=pltpu.SMEM)]
        + [pl.BlockSpec(memory_space=pltpu.VMEM)] * 9,
        out_specs=[pl.BlockSpec(memory_space=pltpu.VMEM)] * 8,
        scratch_shapes=[pltpu.VMEM((3 * DT, 8 * ROWS), jnp.bfloat16), pltpu.VMEM((ROWS, 8 * ROWS), jnp.bfloat16)],
        compiler_params=pltpu.CompilerParams(vmem_limit_bytes=VMEM),
        cost_estimate=pl.CostEstimate(
            flops=24 * DT * ROWS * 8 * ROWS, bytes_accessed=(8 << 20) + 48 * DT * ROWS, transcendentals=0
        ),
        name="project",
    )(order, hidden, *weights)
    return outs[:4], outs[4:]


def add_kernel(first, second, third, fourth, out):
    out[...] = ((first[...] + second[...]) + (third[...] + fourth[...])).astype(jnp.bfloat16)


def add_parts(parts):
    moved = [parts[0]] + [lax.ppermute(parts[step], "y", back(step)) for step in (1, 2, 3)]
    return pl.pallas_call(
        add_kernel,
        out_shape=jax.ShapeDtypeStruct(parts[0].shape, jnp.bfloat16),
        in_specs=[pl.BlockSpec(memory_space=pltpu.VMEM)] * 4,
        out_specs=pl.BlockSpec(memory_space=pltpu.VMEM),
        name="add_parts",
    )(*moved)


def join_kernel(mine, theirs, partners, student, out):
    out[0, :DT, :] = mine[...]
    out[0, DT : 2 * DT, :] = theirs[DT:, :]
    out[1, : 2 * DT, :] = partners[...]
    out[:, 2 * DT :, :] = student[...]


def join(mine, theirs, partners, student):
    return pl.pallas_call(
        join_kernel,
        out_shape=jax.ShapeDtypeStruct((2, 2 * DT + 2 * DS, ROWS), jnp.bfloat16),
        in_specs=[pl.BlockSpec(memory_space=pltpu.VMEM)] * 4,
        out_specs=pl.BlockSpec(memory_space=pltpu.VMEM),
        name="join",
    )(mine, theirs, partners, student)


def fill_units(vectors, units):
    tch, tok, sch, sok = units
    zero = jnp.zeros((), jnp.bfloat16)
    t_pad = jnp.where(lax.broadcasted_iota(jnp.int32, (256 - DT, ROWS), 0) == 0, 1.0, 0.0).astype(jnp.bfloat16)
    s_pad = jnp.where(lax.broadcasted_iota(jnp.int32, (128 - DS, ROWS), 0) == 0, 1.0, 0.0).astype(jnp.bfloat16)
    for slot in range(SLOTS):
        for sub in range(2):
            for head in range(2):
                unit = (slot * 2 + sub) * 2 + head
                t = vectors[slot][sub, head * DT : (head + 1) * DT, :]
                s = vectors[slot][sub, 2 * DT + head * DS : 2 * DT + (head + 1) * DS, :]
                tch[unit, :DT, :] = t
                tch[unit, DT:, :] = t_pad
                sch[unit, :DS, :] = s
                sch[unit, DS:, :] = s_pad
                tok[unit] = jnp.concatenate([t, jnp.zeros((256 - DT, ROWS), jnp.bfloat16)], axis=0).T
                sok[unit] = jnp.concatenate([s, jnp.zeros((128 - DS, ROWS), jnp.bfloat16)], axis=0).T
    tch[NO_UNIT] = jnp.full((256, ROWS), zero)
    sch[NO_UNIT] = jnp.full((128, ROWS), zero)
    t_column = lax.broadcasted_iota(jnp.int32, (ROWS, 256), 1) == DT
    s_column = lax.broadcasted_iota(jnp.int32, (ROWS, 128), 1) == DS
    tok[NO_UNIT] = jnp.where(t_column, LOWEST, 0.0).astype(jnp.bfloat16)
    sok[NO_UNIT] = jnp.where(s_column, LOWEST, 0.0).astype(jnp.bfloat16)


def score(units, query, key):
    tch, tok, sch, sok = units
    return (
        jnp.dot(tok[key], tch[query], preferred_element_type=jnp.float32),
        jnp.dot(sok[key], sch[query], preferred_element_type=jnp.float32),
    )


def diagonal_scores(units, unit):
    t, s = score(units, unit, unit)
    visible = lax.broadcasted_iota(jnp.int32, (ROWS, ROWS), 0) <= lax.broadcasted_iota(jnp.int32, (ROWS, ROWS), 1)
    return jnp.where(visible, t, LOWEST), jnp.where(visible, s, LOWEST)


def walk(tasks, units, buffers, use):
    pairs = tasks[0]

    def load(task, buffer):
        query = tasks[1 + 3 * task]
        for half in range(2):
            t, s = score(units, query, tasks[2 + half + 3 * task])
            buffer[0, half * ROWS : (half + 1) * ROWS, :] = t
            buffer[1, half * ROWS : (half + 1) * ROWS, :] = s

    def take(task, buffer):
        use(tasks[1 + 3 * task], (tasks[2 + 3 * task], tasks[3 + 3 * task]), buffer)

    load(0, buffers[0])

    def two(pair, carry):
        load(2 * pair + 1, buffers[1])
        take(2 * pair, buffers[0])
        load(jnp.minimum(2 * pair + 2, 2 * pairs - 1), buffers[0])
        take(2 * pair + 1, buffers[1])
        return carry

    lax.fori_loop(0, pairs, two, 0)


def add_scores(stats, query, t, s):
    t = t * (TEACHER_SCALE * LOG2E)
    s = s * (STUDENT_SCALE * LOG2E)
    old = stats[query]
    t_peak = jnp.maximum(jnp.max(t, axis=0, keepdims=True), old[0:1])
    s_peak = jnp.maximum(jnp.max(s, axis=0, keepdims=True), old[1:2])
    t_terms = jnp.exp2(t - t_peak)
    s_terms = jnp.exp2(s - s_peak)
    t_decay = jnp.exp2(old[0:1] - t_peak)
    s_decay = jnp.exp2(old[1:2] - s_peak)
    stats[query, 0:1, :] = t_peak
    stats[query, 1:2, :] = s_peak
    stats[query, 2:3, :] = old[2:3] * t_decay + jnp.sum(t_terms, axis=0, keepdims=True)
    stats[query, 3:4, :] = old[3:4] * s_decay + jnp.sum(s_terms, axis=0, keepdims=True)
    stats[query, 4:5, :] = old[4:5] * t_decay + jnp.sum(t_terms * (t - s), axis=0, keepdims=True)


DIAGONAL = (0, 2, 1)
ROW_UNITS = (0, 1)
COLUMN_UNITS = (2, 1)


def stats_kernel(tasks, *refs):
    vectors = refs[:SLOTS]
    along_row, along_column = refs[SLOTS : SLOTS + 2]
    rest = refs[SLOTS + 2 :]
    units, stats, buffers = rest[:4], rest[4], rest[5:]
    fill_units(vectors, units)
    for unit in range(UNITS + 1):
        stats[unit, 0:2, :] = jnp.full((2, ROWS), LOWEST, jnp.float32)
        stats[unit, 2:8, :] = jnp.zeros((6, ROWS), jnp.float32)
    for unit in DIAGONAL:
        add_scores(stats, unit, *diagonal_scores(units, unit))
    walk(tasks, units, buffers, lambda query, keys, buffer: add_scores(stats, query, buffer[0], buffer[1]))
    for step in range(4):
        for out, slot, chosen in (
            (along_row, step, ROW_UNITS),
            (along_column, 3 + step if step else 0, COLUMN_UNITS),
        ):
            for place, unit in enumerate(chosen):
                first = (step * 2 + place) * 8
                out[first : first + 8, :] = stats[slot * 4 + unit]


UNIT_SCRATCH = [
    ((UNITS + 1, 256, ROWS), jnp.bfloat16),
    ((UNITS + 1, ROWS, 256), jnp.bfloat16),
    ((UNITS + 1, 128, ROWS), jnp.bfloat16),
    ((UNITS + 1, ROWS, 128), jnp.bfloat16),
]
BUFFERS = [((2, 2 * ROWS, ROWS), jnp.float32)] * 2


def row_stats(tasks, vectors):
    scratch = UNIT_SCRATCH + [((UNITS + 1, 8, ROWS), jnp.float32)] + BUFFERS
    return pl.pallas_call(
        stats_kernel,
        out_shape=[jax.ShapeDtypeStruct((64, ROWS), jnp.float32)] * 2,
        in_specs=[pl.BlockSpec(memory_space=pltpu.SMEM)] + [pl.BlockSpec(memory_space=pltpu.VMEM)] * SLOTS,
        out_specs=[pl.BlockSpec(memory_space=pltpu.VMEM)] * 2,
        scratch_shapes=[pltpu.VMEM(s, d) for s, d in scratch],
        compiler_params=pltpu.CompilerParams(vmem_limit_bytes=VMEM),
        name="row_stats",
    )(tasks, *vectors)


def merge_rows(parts):
    t_peak, s_peak = parts[0][0:1], parts[0][1:2]
    for part in parts[1:]:
        t_peak = jnp.maximum(t_peak, part[0:1])
        s_peak = jnp.maximum(s_peak, part[1:2])
    t_mass = s_mass = weighted = jnp.zeros((1, ROWS), jnp.float32)
    for part in parts:
        t_decay = jnp.exp2(part[0:1] - t_peak)
        t_mass = t_mass + part[2:3] * t_decay
        s_mass = s_mass + part[3:4] * jnp.exp2(part[1:2] - s_peak)
        weighted = weighted + part[4:5] * t_decay
    t_total = t_peak + jnp.log(t_mass) * LOG2E
    s_total = s_peak + jnp.log(s_mass) * LOG2E
    return t_total, s_total, (weighted / t_mass - t_total + s_total) * LN2


def merge_parts(rows, columns, total, divergence):
    def of(line, step, place):
        entries = [((step - ahead) % 4 * 2 + place) * 8 for ahead in range(4)]
        return [part[entry : entry + 8, :] for part, entry in zip(line, entries)]

    divergence[...] = jnp.zeros((8, ROWS), jnp.float32)
    cases = [(0, 0, of(rows, 0, 0)), (0, 2, of(columns, 0, 0)), (0, 1, of(rows, 0, 1) + of(columns, 0, 1)[1:])]
    for step in (1, 2, 3):
        cases += [(step, unit, of(rows, step, place)) for place, unit in enumerate(ROW_UNITS)]
        cases += [(3 + step, unit, of(columns, step, place)) for place, unit in enumerate(COLUMN_UNITS)]
    for index, (slot, unit, parts) in enumerate(cases):
        t_total, s_total, value = merge_rows(parts)
        total[slot * 4 + unit, 0:1, :] = t_total
        total[slot * 4 + unit, 1:2, :] = s_total
        if index < 3:
            divergence[index : index + 1, :] = value


def grad_kernel(tasks, *refs):
    vectors, refs = refs[:SLOTS], refs[SLOTS:]
    rows, columns, outs, divergence = refs[:4], refs[4:8], refs[8 : 8 + SLOTS], refs[8 + SLOTS]
    rest = refs[9 + SLOTS :]
    units, total, grad, buffers = rest[:4], rest[4], rest[5], rest[6:]
    fill_units(vectors, units)
    sch = units[2]
    merge_parts(rows, columns, total, divergence)
    total[NO_UNIT] = jnp.full((8, ROWS), -LOWEST, jnp.float32)
    grad[...] = jnp.zeros((UNITS + 1, DS, ROWS), jnp.float32)

    def add(query, key, t, s):
        t_prob = jnp.exp2(t * (TEACHER_SCALE * LOG2E) - total[query, 0:1, :])
        s_prob = jnp.exp2(s * (STUDENT_SCALE * LOG2E) - total[query, 1:2, :])
        weights = ((s_prob - t_prob) * STUDENT_SCALE).astype(jnp.bfloat16)
        grad[query] += jnp.dot(sch[key, :DS, :], weights, preferred_element_type=jnp.float32)
        grad[key] += lax.dot_general(
            sch[query, :DS, :], weights, (((1,), (1,)), ((), ())), preferred_element_type=jnp.float32
        )

    def use(query, keys, buffer):
        for half in range(2):
            part = slice(half * ROWS, (half + 1) * ROWS)
            add(query, keys[half], buffer[0, part, :], buffer[1, part, :])

    for unit in DIAGONAL:
        add(unit, unit, *diagonal_scores(units, unit))
    walk(tasks, units, buffers, use)
    for slot in range(SLOTS):
        for unit in range(4):
            outs[slot][unit * DS : (unit + 1) * DS, :] = grad[slot * 4 + unit]


def gradients(tasks, vectors, rows, columns):
    scratch = UNIT_SCRATCH + [((UNITS + 1, 8, ROWS), jnp.float32), ((UNITS + 1, DS, ROWS), jnp.float32)] + BUFFERS
    outs = pl.pallas_call(
        grad_kernel,
        out_shape=[jax.ShapeDtypeStruct((4 * DS, ROWS), jnp.float32)] * SLOTS
        + [jax.ShapeDtypeStruct((8, ROWS), jnp.float32)],
        in_specs=[pl.BlockSpec(memory_space=pltpu.SMEM)] + [pl.BlockSpec(memory_space=pltpu.VMEM)] * (SLOTS + 8),
        out_specs=[pl.BlockSpec(memory_space=pltpu.VMEM)] * (SLOTS + 1),
        scratch_shapes=[pltpu.VMEM(s, d) for s, d in scratch],
        compiler_params=pltpu.CompilerParams(vmem_limit_bytes=VMEM),
        name="gradients",
    )(tasks, *vectors, *rows, *columns)
    return outs[:SLOTS], outs[SLOTS]


def to_line(block, axis):
    return [block] + [lax.ppermute(block, axis, back(step)) for step in (1, 2, 3)]


def pair_students(student, zh):
    heads = student.reshape(3, DS, ROWS)
    mine = jnp.concatenate([jnp.where(zh == 0, heads[0], heads[1]), heads[2]], axis=0)
    theirs = jnp.concatenate([jnp.where(zh == 0, heads[1], heads[0]), heads[2]], axis=0)
    return jnp.stack([mine, lax.ppermute(theirs, "zh", SWAP)])


def shards(hidden, q_weight, regroup, student_rel):
    x, zh, y = lax.axis_index("x"), lax.axis_index("zh"), lax.axis_index("y")
    head = lax.axis_index(HEAD)
    place = x * 8 + zh * 4 + y
    tasks = lax.dynamic_index_in_dim(jnp.asarray(plan()), place, 0, keepdims=False)

    zl, core = lax.axis_index("zl"), lax.axis_index("core")
    line = to_line(q_weight.T, "zl")
    columns = line + [lax.ppermute(piece, "core", SWAP) for piece in line]
    owners = (zl + jnp.arange(4, dtype=jnp.int32)) % 4 * 2
    bases = jnp.concatenate([owners + core, owners + 1 - core]) * columns[0].shape[0]

    quarters = [lax.dynamic_slice(hidden, (0, (y + step) % 4 * ROWS), (ROWS, ROWS)) for step in range(4)]
    quarters = quarters[:1] + [lax.ppermute(quarters[step], "y", forth(step)) for step in (1, 2, 3)]
    features = lax.all_gather(stack(quarters, line[1:2]), HEAD, axis=0)

    pair = pair_students(student_rel.T, zh)
    channels = lax.dynamic_slice_in_dim(regroup, head * (3 * DT), 3 * DT, 0)
    chosen = choose(bases, channels[:, None], columns, (pair,))
    other = lax.ppermute(chosen, "zh", SWAP)
    pieces = to_line(chosen, "x") + to_line(other, "x")
    around = (x + jnp.arange(4, dtype=jnp.int32)) % 4 * 2
    order = jnp.concatenate([around + zh, around + 1 - zh, zh.reshape(1)])

    theirs, mine = project(order, features, pieces)
    theirs = add_parts(theirs)
    partners = lax.ppermute(theirs, "zh", SWAP)
    vectors = to_slots(join(add_parts(mine), theirs, partners, pair))

    along_row, along_column = row_stats(tasks, vectors)
    grads, divergence = gradients(tasks, vectors, to_line(along_row, "y"), to_line(along_column, "x"))
    grads = to_owners(grads)
    grad = grads[0]
    for piece in grads[1:]:
        grad = grad + piece

    swapped = lax.ppermute(grad[2 * DS :], "zh", SWAP)
    first = jnp.where(zh == 0, grad[:DS], swapped[:DS])
    second = jnp.where(zh == 0, swapped[:DS], grad[:DS])
    third = grad[DS : 2 * DS] + swapped[DS:]
    student_grad = jnp.concatenate([first, second, third], axis=0).T

    away = lax.ppermute(divergence[1:2], "zh", SWAP)[0]
    first = jnp.where(zh == 0, divergence[0], away)
    second = jnp.where(zh == 0, away, divergence[0])
    return student_grad, jnp.stack([first, second, divergence[2]], axis=1)


def solution(mesh):
    whole = Mesh(mesh.devices.reshape(4, 2, 4, 4, 2), CTX + HEAD)
    split = P(CTX, HEAD)
    return jax.shard_map(
        shards,
        mesh=whole,
        in_specs=(split, split, P(), split),
        out_specs=(split, split),
        check_vma=False,
    )
```

```python
import jax
import jax.numpy as jnp
import numpy as np
from jax import lax
from jax.experimental import pallas as pl
from jax.experimental.pallas import tpu as pltpu
from jax.sharding import Mesh
from jax.sharding import PartitionSpec as P

R = 24
DT = 176
DS = 32
TQ = 4096
ROWS = 256
SLOTS = 7
UNITS = SLOTS * 4
NO_UNIT = UNITS
LOG2E = 1.4426950408889634
LN2 = 0.6931471805599453
TEACHER_SCALE = 1.0 / DT**0.5
STUDENT_SCALE = 1.0 / DS**0.5
LOG2_SCALE = -2.5
LOWEST = -3.0e38
CHUNK = 32
VMEM = 48 * 1024 * 1024
CTX = ("x", "zh", "y")
HEAD = ("zl", "core")


def back(step):
    return [(src, (src - step) % 4) for src in range(4)]


def forth(step):
    return [(src, (src + step) % 4) for src in range(4)]


SWAP = [(0, 1), (1, 0)]


def to_slots(block):
    rows = [lax.ppermute(block, "y", back(step)) for step in (1, 2, 3)]
    columns = [lax.ppermute(block, "x", back(step)) for step in (1, 2, 3)]
    return [block] + rows + columns


def to_owners(slots):
    rows = [lax.ppermute(slots[step], "y", forth(step)) for step in (1, 2, 3)]
    columns = [lax.ppermute(slots[3 + step], "x", forth(step)) for step in (1, 2, 3)]
    return [slots[0]] + rows + columns


def slot_of(device, block):
    (x, y), (bx, by) = device, block
    if bx == x:
        return (by - y) % 4
    return 3 + (bx - x) % 4


def holds(device, block):
    return device[0] == block[0] or device[1] == block[1]


def by_row(x, y, sub, head):
    return sub == 0 if head == 0 else (x + y) % 2 == 0


def plan():
    places = [(x, y) for x in range(4) for y in range(4)]
    table = np.zeros((4, 2, 4, 256), np.int32)

    def where(chunk):
        return (chunk // 8, chunk % 4), (chunk // 4) % 2

    for zh in range(2):
        load = {place: 0 for place in places}
        keys_of = {place: {} for place in places}
        open_tiles = []
        for head in range(2):
            for query in range(32):
                block, half = where(query)
                sub = 0 if half == zh else 1
                if head == 1 and sub == 1:
                    continue
                line = 0 if by_row(*block, sub, head) else 1
                for key in range(query):
                    spots = [
                        d for d in places if d[line] == block[line] and holds(d, block) and holds(d, where(key)[0])
                    ]
                    open_tiles.append((len(spots), head, query, key, spots))
        open_tiles.sort(key=lambda tile: tile[:4])
        for _, head, query, key, spots in open_tiles:
            odd = {d: len(keys_of[d].get((head, query), ())) % 2 for d in spots}
            best = min(spots, key=lambda d: (load[d] - odd[d], d))
            load[best] += 1
            keys_of[best].setdefault((head, query), []).append(key)
        for place in places:
            x, y = place

            def unit(head, chunk):
                block, half = where(chunk)
                return (slot_of(place, block) * 2 + (0 if half == zh else 1)) * 2 + head

            tasks = []
            for (head, query), keys in sorted(keys_of[place].items()):
                units = [unit(head, key) for key in sorted(keys)]
                if len(units) % 2:
                    units.append(NO_UNIT)
                tasks += [(unit(head, query), a, b) for a, b in zip(units[::2], units[1::2])]
            if len(tasks) % 2:
                tasks.append((NO_UNIT, NO_UNIT, NO_UNIT))
            row = table[x, zh, y]
            row[0] = len(tasks) // 2
            for index, task in enumerate(tasks):
                row[1 + 3 * index : 4 + 3 * index] = task
    return table.reshape(32, 256)


def hold_kernel(value, after, out):
    out[...] = value[...]


def hold(value, after):
    return pl.pallas_call(
        hold_kernel,
        out_shape=jax.ShapeDtypeStruct(value.shape, value.dtype),
        in_specs=[pl.BlockSpec(memory_space=pltpu.VMEM), pl.BlockSpec(memory_space=pl.ANY)],
        out_specs=pl.BlockSpec(memory_space=pltpu.VMEM),
        name="hold",
    )(value, after)


def choose_kernel(bases, channels, *refs):
    pieces, out = refs[:8], refs[-1]
    for head in range(3):
        rows = slice(head * DT, (head + 1) * DT)
        total = None
        for index, piece in enumerate(pieces):
            places = lax.broadcasted_iota(jnp.int32, (DT, piece.shape[0]), 1)
            picked = jnp.where(channels[rows, :] - bases[index] == places, 1.0, 0.0).astype(jnp.bfloat16)
            part = jnp.dot(picked, piece[...], preferred_element_type=jnp.float32)
            total = part if total is None else total + part
        out[rows, :] = total.astype(jnp.bfloat16)


def choose(bases, channels, pieces, after):
    size = channels.shape[0]
    return pl.pallas_call(
        choose_kernel,
        out_shape=jax.ShapeDtypeStruct((size, ROWS), jnp.bfloat16),
        in_specs=[pl.BlockSpec(memory_space=pltpu.SMEM)]
        + [pl.BlockSpec(memory_space=pltpu.VMEM)] * 9
        + [pl.BlockSpec(memory_space=pl.ANY)] * len(after),
        out_specs=pl.BlockSpec(memory_space=pltpu.VMEM),
        compiler_params=pltpu.CompilerParams(vmem_limit_bytes=VMEM),
        cost_estimate=pl.CostEstimate(flops=2 * size * ROWS * TQ, bytes_accessed=3 << 20, transcendentals=0),
        name="choose",
    )(bases, channels, *pieces, *after)


def project_kernel(order, hidden, *refs):
    weights, outs, (wide, tall) = refs[:8], refs[-10:-2], refs[-2:]
    zh = order[8]
    for piece in range(8):
        columns = slice(piece * ROWS, (piece + 1) * ROWS)
        for place, head in enumerate((1 - zh, 2, zh)):
            rows = pl.ds(pl.multiple_of(head * DT, 16), DT)
            wide[place * DT : (place + 1) * DT, columns] = weights[piece][rows, :]
    for block in (2, 1, 3, 0):
        for piece in range(8):
            tall[:, piece * ROWS : (piece + 1) * ROWS] = hidden[order[piece], block * ROWS : (block + 1) * ROWS, :]
        for out, rows in ((outs[block], slice(0, 2 * DT)), (outs[4 + block], slice(2 * DT, 3 * DT))):
            out[...] = lax.dot_general(
                wide[rows, :], tall[...], (((1,), (1,)), ((), ())), preferred_element_type=jnp.float32
            )


def project(order, hidden, weights):
    sizes = [2 * DT] * 4 + [DT] * 4
    outs = pl.pallas_call(
        project_kernel,
        out_shape=[jax.ShapeDtypeStruct((size, ROWS), jnp.float32) for size in sizes],
        in_specs=[pl.BlockSpec(memory_space=pltpu.SMEM)]
        + [pl.BlockSpec(memory_space=pltpu.VMEM)] * 9,
        out_specs=[pl.BlockSpec(memory_space=pltpu.VMEM)] * 8,
        scratch_shapes=[pltpu.VMEM((3 * DT, 8 * ROWS), jnp.bfloat16), pltpu.VMEM((ROWS, 8 * ROWS), jnp.bfloat16)],
        compiler_params=pltpu.CompilerParams(vmem_limit_bytes=VMEM),
        cost_estimate=pl.CostEstimate(
            flops=24 * DT * ROWS * 8 * ROWS, bytes_accessed=(8 << 20) + 48 * DT * ROWS, transcendentals=0
        ),
        name="project",
    )(order, hidden, *weights)
    return outs[:4], outs[4:]


def add_parts(parts):
    moved = [lax.ppermute(parts[step], "y", back(step)) for step in (1, 2, 3)]
    return ((parts[0] + moved[0]) + (moved[1] + moved[2])).astype(jnp.bfloat16)


def join(mine, theirs, partners, student):
    return jnp.stack(
        [
            jnp.concatenate([mine, theirs[DT:], student[0]], axis=0),
            jnp.concatenate([partners, student[1]], axis=0),
        ]
    )


def fill_units(vectors, units):
    tch, tok, sch, sok = units
    zero = jnp.zeros((), jnp.bfloat16)
    t_pad = jnp.where(lax.broadcasted_iota(jnp.int32, (256 - DT, ROWS), 0) == 0, 1.0, 0.0).astype(jnp.bfloat16)
    s_pad = jnp.where(lax.broadcasted_iota(jnp.int32, (128 - DS, ROWS), 0) == 0, 1.0, 0.0).astype(jnp.bfloat16)
    for slot in range(SLOTS):
        for sub in range(2):
            for head in range(2):
                unit = (slot * 2 + sub) * 2 + head
                t = vectors[slot][sub, head * DT : (head + 1) * DT, :]
                s = vectors[slot][sub, 2 * DT + head * DS : 2 * DT + (head + 1) * DS, :]
                tch[unit, :DT, :] = t
                tch[unit, DT:, :] = t_pad
                sch[unit, :DS, :] = s
                sch[unit, DS:, :] = s_pad
                tok[unit] = jnp.concatenate([t, jnp.zeros((256 - DT, ROWS), jnp.bfloat16)], axis=0).T
                sok[unit] = jnp.concatenate([s, jnp.zeros((128 - DS, ROWS), jnp.bfloat16)], axis=0).T
    tch[NO_UNIT] = jnp.full((256, ROWS), zero)
    sch[NO_UNIT] = jnp.full((128, ROWS), zero)
    t_column = lax.broadcasted_iota(jnp.int32, (ROWS, 256), 1) == DT
    s_column = lax.broadcasted_iota(jnp.int32, (ROWS, 128), 1) == DS
    tok[NO_UNIT] = jnp.where(t_column, LOWEST, 0.0).astype(jnp.bfloat16)
    sok[NO_UNIT] = jnp.where(s_column, LOWEST, 0.0).astype(jnp.bfloat16)


def score(units, query, key):
    tch, tok, sch, sok = units
    return (
        jnp.dot(tok[key], tch[query], preferred_element_type=jnp.float32),
        jnp.dot(sok[key], sch[query], preferred_element_type=jnp.float32),
    )


def diagonal_scores(units, unit):
    t, s = score(units, unit, unit)
    visible = lax.broadcasted_iota(jnp.int32, (ROWS, ROWS), 0) <= lax.broadcasted_iota(jnp.int32, (ROWS, ROWS), 1)
    t = jnp.where(visible, t * (TEACHER_SCALE * LOG2E), LOWEST)
    return t, jnp.where(visible, s * (STUDENT_SCALE * LOG2E), LOWEST)


def walk(tasks, units, buffers, use):
    pairs = tasks[0]

    def load(task, buffer):
        query = tasks[1 + 3 * task]
        for half in range(2):
            t, s = score(units, query, tasks[2 + half + 3 * task])
            buffer[0, half * ROWS : (half + 1) * ROWS, :] = t * (TEACHER_SCALE * LOG2E)
            buffer[1, half * ROWS : (half + 1) * ROWS, :] = s * (STUDENT_SCALE * LOG2E)

    def take(task, buffer):
        use(tasks[1 + 3 * task], (tasks[2 + 3 * task], tasks[3 + 3 * task]), buffer)

    load(0, buffers[0])

    def two(pair, carry):
        load(2 * pair + 1, buffers[1])
        take(2 * pair, buffers[0])
        load(jnp.minimum(2 * pair + 2, 2 * pairs - 1), buffers[0])
        take(2 * pair + 1, buffers[1])
        return carry

    lax.fori_loop(0, pairs, two, 0)


def add_scores(stats, query, scores):
    old = stats[query]
    parts = [slice(start, start + CHUNK) for start in range(0, scores.shape[1], CHUNK)]

    def fold(values, combine):
        return combine(values.reshape(CHUNK // 8, 8, ROWS), axis=0)

    t_peak = s_peak = jnp.full((8, ROWS), LOWEST, jnp.float32)
    for part in parts:
        t_peak = jnp.maximum(t_peak, fold(scores[0, part, :], jnp.max))
        s_peak = jnp.maximum(s_peak, fold(scores[1, part, :], jnp.max))
    t_peak = jnp.maximum(jnp.max(t_peak, axis=0, keepdims=True), old[0:1])
    s_peak = jnp.maximum(jnp.max(s_peak, axis=0, keepdims=True), old[1:2])
    t_mass = s_mass = weighted = jnp.zeros((8, ROWS), jnp.float32)
    for part in parts:
        t, s = scores[0, part, :], scores[1, part, :]
        t_terms = jnp.exp2(t - t_peak)
        t_mass = t_mass + fold(t_terms, jnp.sum)
        weighted = weighted + fold(t_terms * (t - s), jnp.sum)
        s_mass = s_mass + fold(jnp.exp2(s - s_peak), jnp.sum)
    t_decay = jnp.exp2(old[0:1] - t_peak)
    s_decay = jnp.exp2(old[1:2] - s_peak)
    stats[query, 0:1, :] = t_peak
    stats[query, 1:2, :] = s_peak
    stats[query, 2:3, :] = old[2:3] * t_decay + jnp.sum(t_mass, axis=0, keepdims=True)
    stats[query, 3:4, :] = old[3:4] * s_decay + jnp.sum(s_mass, axis=0, keepdims=True)
    stats[query, 4:5, :] = old[4:5] * t_decay + jnp.sum(weighted, axis=0, keepdims=True)


DIAGONAL = (0, 2, 1)
ROW_UNITS = (0, 1)
COLUMN_UNITS = (2, 1)


def stats_kernel(tasks, *refs):
    vectors = refs[:SLOTS]
    along_row, along_column = refs[SLOTS : SLOTS + 2]
    rest = refs[SLOTS + 2 :]
    units, stats, buffers = rest[:4], rest[4], rest[5:]
    fill_units(vectors, units)
    for unit in range(UNITS + 1):
        stats[unit, 0:2, :] = jnp.full((2, ROWS), LOWEST, jnp.float32)
        stats[unit, 2:8, :] = jnp.zeros((6, ROWS), jnp.float32)
    for unit in DIAGONAL:
        block = buffers[0].at[:, :ROWS, :]
        block[0], block[1] = diagonal_scores(units, unit)
        add_scores(stats, unit, block)
    walk(tasks, units, buffers, lambda query, keys, buffer: add_scores(stats, query, buffer))
    for step in range(4):
        for out, slot, chosen in (
            (along_row, step, ROW_UNITS),
            (along_column, 3 + step if step else 0, COLUMN_UNITS),
        ):
            for place, unit in enumerate(chosen):
                first = (step * 2 + place) * 8
                out[first : first + 8, :] = stats[slot * 4 + unit]


UNIT_SCRATCH = [
    ((UNITS + 1, 256, ROWS), jnp.bfloat16),
    ((UNITS + 1, ROWS, 256), jnp.bfloat16),
    ((UNITS + 1, 128, ROWS), jnp.bfloat16),
    ((UNITS + 1, ROWS, 128), jnp.bfloat16),
]
BUFFERS = [((2, 2 * ROWS, ROWS), jnp.float32)] * 2


def row_stats(tasks, vectors):
    scratch = UNIT_SCRATCH + [((UNITS + 1, 8, ROWS), jnp.float32)] + BUFFERS
    return pl.pallas_call(
        stats_kernel,
        out_shape=[jax.ShapeDtypeStruct((64, ROWS), jnp.float32)] * 2,
        in_specs=[pl.BlockSpec(memory_space=pltpu.SMEM)] + [pl.BlockSpec(memory_space=pltpu.VMEM)] * SLOTS,
        out_specs=[pl.BlockSpec(memory_space=pltpu.VMEM)] * 2,
        scratch_shapes=[pltpu.VMEM(s, d) for s, d in scratch],
        compiler_params=pltpu.CompilerParams(vmem_limit_bytes=VMEM),
        name="row_stats",
    )(tasks, *vectors)


def merge_rows(parts):
    t_peak, s_peak = parts[0][0:1], parts[0][1:2]
    for part in parts[1:]:
        t_peak = jnp.maximum(t_peak, part[0:1])
        s_peak = jnp.maximum(s_peak, part[1:2])
    t_mass = s_mass = weighted = jnp.zeros((1, ROWS), jnp.float32)
    for part in parts:
        t_decay = jnp.exp2(part[0:1] - t_peak)
        t_mass = t_mass + part[2:3] * t_decay
        s_mass = s_mass + part[3:4] * jnp.exp2(part[1:2] - s_peak)
        weighted = weighted + part[4:5] * t_decay
    t_total = t_peak + jnp.log(t_mass) * LOG2E
    s_total = s_peak + jnp.log(s_mass) * LOG2E
    return t_total, s_total, (weighted / t_mass - t_total + s_total) * LN2


def merge_parts(rows, columns, total, divergence):
    def of(line, step, place):
        entries = [((step - ahead) % 4 * 2 + place) * 8 for ahead in range(4)]
        return [part[entry : entry + 8, :] for part, entry in zip(line, entries)]

    divergence[...] = jnp.zeros((8, ROWS), jnp.float32)
    cases = [(0, 0, of(rows, 0, 0)), (0, 2, of(columns, 0, 0)), (0, 1, of(rows, 0, 1) + of(columns, 0, 1)[1:])]
    for step in (1, 2, 3):
        cases += [(step, unit, of(rows, step, place)) for place, unit in enumerate(ROW_UNITS)]
        cases += [(3 + step, unit, of(columns, step, place)) for place, unit in enumerate(COLUMN_UNITS)]
    for index, (slot, unit, parts) in enumerate(cases):
        t_total, s_total, value = merge_rows(parts)
        total[slot * 4 + unit, 0:1, :] = t_total - LOG2_SCALE
        total[slot * 4 + unit, 1:2, :] = s_total - LOG2_SCALE
        if index < 3:
            divergence[index : index + 1, :] = value


def grad_kernel(tasks, *refs):
    vectors, refs = refs[:SLOTS], refs[SLOTS:]
    rows, columns, outs, divergence = refs[:4], refs[4:8], refs[8 : 8 + SLOTS], refs[8 + SLOTS]
    rest = refs[9 + SLOTS :]
    units, total, grad, buffers = rest[:4], rest[4], rest[5], rest[6:]
    fill_units(vectors, units)
    sch = units[2]
    merge_parts(rows, columns, total, divergence)
    total[NO_UNIT] = jnp.full((8, ROWS), -LOWEST, jnp.float32)
    grad[...] = jnp.zeros((UNITS + 1, DS, ROWS), jnp.float32)

    def add(query, key, t, s):
        t_prob = jnp.exp2(t - total[query, 0:1, :])
        s_prob = jnp.exp2(s - total[query, 1:2, :])
        weights = (s_prob - t_prob).astype(jnp.bfloat16)
        grad[query] += jnp.dot(sch[key, :DS, :], weights, preferred_element_type=jnp.float32)
        grad[key] += lax.dot_general(
            sch[query, :DS, :], weights, (((1,), (1,)), ((), ())), preferred_element_type=jnp.float32
        )

    def use(query, keys, buffer):
        for half in range(2):
            part = slice(half * ROWS, (half + 1) * ROWS)
            add(query, keys[half], buffer[0, part, :], buffer[1, part, :])

    for unit in DIAGONAL:
        add(unit, unit, *diagonal_scores(units, unit))
    walk(tasks, units, buffers, use)
    for slot in range(SLOTS):
        for unit in range(4):
            outs[slot][unit * DS : (unit + 1) * DS, :] = grad[slot * 4 + unit]


def gradients(tasks, vectors, rows, columns):
    scratch = UNIT_SCRATCH + [((UNITS + 1, 8, ROWS), jnp.float32), ((UNITS + 1, DS, ROWS), jnp.float32)] + BUFFERS
    outs = pl.pallas_call(
        grad_kernel,
        out_shape=[jax.ShapeDtypeStruct((4 * DS, ROWS), jnp.float32)] * SLOTS
        + [jax.ShapeDtypeStruct((8, ROWS), jnp.float32)],
        in_specs=[pl.BlockSpec(memory_space=pltpu.SMEM)] + [pl.BlockSpec(memory_space=pltpu.VMEM)] * (SLOTS + 8),
        out_specs=[pl.BlockSpec(memory_space=pltpu.VMEM)] * (SLOTS + 1),
        scratch_shapes=[pltpu.VMEM(s, d) for s, d in scratch],
        compiler_params=pltpu.CompilerParams(vmem_limit_bytes=VMEM),
        name="gradients",
    )(tasks, *vectors, *rows, *columns)
    return outs[:SLOTS], outs[SLOTS]


def to_line(block, axis):
    return [block] + [lax.ppermute(block, axis, back(step)) for step in (1, 2, 3)]


def pair_students(student, zh):
    heads = student.reshape(3, DS, ROWS)
    mine = jnp.concatenate([jnp.where(zh == 0, heads[0], heads[1]), heads[2]], axis=0)
    theirs = jnp.concatenate([jnp.where(zh == 0, heads[1], heads[0]), heads[2]], axis=0)
    return jnp.stack([mine, lax.ppermute(theirs, "zh", SWAP)])


def shards(hidden, q_weight, regroup, student_rel):
    x, zh, y = lax.axis_index("x"), lax.axis_index("zh"), lax.axis_index("y")
    head = lax.axis_index(HEAD)
    place = x * 8 + zh * 4 + y
    tasks = lax.dynamic_index_in_dim(jnp.asarray(plan()), place, 0, keepdims=False)

    zl, core = lax.axis_index("zl"), lax.axis_index("core")
    line = to_line(q_weight.T, "zl")
    columns = line + [lax.ppermute(piece, "core", SWAP) for piece in line]
    owners = (zl + jnp.arange(4, dtype=jnp.int32)) % 4 * 2
    bases = jnp.concatenate([owners + core, owners + 1 - core]) * columns[0].shape[0]

    quarters = [lax.dynamic_slice(hidden, (0, (y + step) % 4 * ROWS), (ROWS, ROWS)) for step in range(4)]
    quarters = quarters[:1] + [lax.ppermute(quarters[step], "y", forth(step)) for step in (1, 2, 3)]
    quarters[0] = hold(quarters[0], line[1])
    features = lax.all_gather(jnp.concatenate(quarters, axis=0), HEAD, axis=0)

    pair = pair_students(student_rel.T, zh)
    channels = lax.dynamic_slice_in_dim(regroup, head * (3 * DT), 3 * DT, 0)
    chosen = choose(bases, channels[:, None], columns, (pair,))
    other = lax.ppermute(chosen, "zh", SWAP)
    pieces = to_line(chosen, "x") + to_line(other, "x")
    around = (x + jnp.arange(4, dtype=jnp.int32)) % 4 * 2
    order = jnp.concatenate([around + zh, around + 1 - zh, zh.reshape(1)])

    theirs, mine = project(order, features, pieces)
    theirs = add_parts(theirs)
    partners = lax.ppermute(theirs, "zh", SWAP)
    vectors = to_slots(join(add_parts(mine), theirs, partners, pair))

    along_row, along_column = row_stats(tasks, vectors)
    grads, divergence = gradients(tasks, vectors, to_line(along_row, "y"), to_line(along_column, "x"))
    grads = to_owners(grads)
    grad = grads[0]
    for piece in grads[1:]:
        grad = grad + piece

    swapped = lax.ppermute(jnp.concatenate([grad[2 * DS :], divergence], axis=0), "zh", SWAP)
    first = jnp.where(zh == 0, grad[:DS], swapped[:DS])
    second = jnp.where(zh == 0, swapped[:DS], grad[:DS])
    third = grad[DS : 2 * DS] + swapped[DS : 2 * DS]
    student_grad = jnp.concatenate([first, second, third], axis=0).T

    away = swapped[2 * DS + 1]
    first = jnp.where(zh == 0, divergence[0], away)
    second = jnp.where(zh == 0, away, divergence[0])
    return student_grad, jnp.stack([first, second, divergence[2]], axis=1)


def solution(mesh):
    whole = Mesh(mesh.devices.reshape(4, 2, 4, 4, 2), CTX + HEAD)
    split = P(CTX, HEAD)
    return jax.shard_map(
        shards,
        mesh=whole,
        in_specs=(split, split, P(), split),
        out_specs=(split, split),
        check_vma=False,
    )
```

```python
import jax
import jax.numpy as jnp
import numpy as np
from jax import lax
from jax.experimental import pallas as pl
from jax.experimental.pallas import tpu as pltpu
from jax.sharding import Mesh
from jax.sharding import PartitionSpec as P

R = 24
DT = 176
DS = 32
TQ = 4096
ROWS = 256
SLOTS = 7
OPERANDS = (0, 2, 5, 3, 6, 1, 4)
UNITS = SLOTS * 4
NO_UNIT = UNITS
LOG2E = 1.4426950408889634
LN2 = 0.6931471805599453
TEACHER_SCALE = 1.0 / DT**0.5
STUDENT_SCALE = 1.0 / DS**0.5
LOG2_SCALE = -2.5
LOWEST = -3.0e38
CHUNK = 32
VMEM = 32 * 1024 * 1024
CTX = ("x", "zh", "y")
HEAD = ("zl", "core")


def back(step):
    return [(src, (src - step) % 4) for src in range(4)]


def forth(step):
    return [(src, (src + step) % 4) for src in range(4)]


SWAP = [(0, 1), (1, 0)]


def to_slots(block):
    rows = [lax.ppermute(block, "y", back(step)) for step in (1, 2, 3)]
    columns = [lax.ppermute(block, "x", back(step)) for step in (1, 2, 3)]
    return [block] + rows + columns


def to_owners(slots):
    rows = [lax.ppermute(slots[step], "y", forth(step)) for step in (1, 2, 3)]
    columns = [lax.ppermute(slots[3 + step], "x", forth(step)) for step in (1, 2, 3)]
    return [slots[0]] + rows + columns


def slot_of(device, block):
    (x, y), (bx, by) = device, block
    if bx == x:
        return (by - y) % 4
    return 3 + (bx - x) % 4


def holds(device, block):
    return device[0] == block[0] or device[1] == block[1]


def by_row(x, y, sub, head):
    return sub == 0 if head == 0 else (x + y) % 2 == 0


def plan():
    places = [(x, y) for x in range(4) for y in range(4)]
    table = np.zeros((4, 2, 4, 256), np.int32)

    def where(chunk):
        return (chunk // 8, chunk % 4), (chunk // 4) % 2

    for zh in range(2):
        load = {place: 0 for place in places}
        keys_of = {place: {} for place in places}
        open_tiles = []
        for head in range(2):
            for query in range(32):
                block, half = where(query)
                sub = 0 if half == zh else 1
                if head == 1 and sub == 1:
                    continue
                line = 0 if by_row(*block, sub, head) else 1
                for key in range(query):
                    spots = [
                        d for d in places if d[line] == block[line] and holds(d, block) and holds(d, where(key)[0])
                    ]
                    open_tiles.append((len(spots), head, query, key, spots))
        open_tiles.sort(key=lambda tile: tile[:4])
        for _, head, query, key, spots in open_tiles:
            odd = {d: len(keys_of[d].get((head, query), ())) % 2 for d in spots}
            best = min(spots, key=lambda d: (load[d] - odd[d], d))
            load[best] += 1
            keys_of[best].setdefault((head, query), []).append(key)
        for place in places:
            x, y = place

            def unit(head, chunk):
                block, half = where(chunk)
                return (slot_of(place, block) * 2 + (0 if half == zh else 1)) * 2 + head

            tasks = []
            for (head, query), keys in sorted(keys_of[place].items()):
                units = [unit(head, key) for key in sorted(keys)]
                if len(units) % 2:
                    units.append(NO_UNIT)
                tasks += [(unit(head, query), a, b) for a, b in zip(units[::2], units[1::2])]
            if len(tasks) % 2:
                tasks.append((NO_UNIT, NO_UNIT, NO_UNIT))
            row = table[x, zh, y]
            row[0] = len(tasks) // 2
            for index, task in enumerate(tasks):
                row[1 + 3 * index : 4 + 3 * index] = task
    return table.reshape(32, 256)


def hold_kernel(value, after, out):
    out[...] = value[...]


def hold(value, after):
    return pl.pallas_call(
        hold_kernel,
        out_shape=jax.ShapeDtypeStruct(value.shape, value.dtype),
        in_specs=[pl.BlockSpec(memory_space=pltpu.VMEM), pl.BlockSpec(memory_space=pl.ANY)],
        out_specs=pl.BlockSpec(memory_space=pltpu.VMEM),
        name="hold",
    )(value, after)


def choose_kernel(bases, channels, *refs):
    pieces, out = refs[:8], refs[-1]
    for head in range(3):
        rows = slice(head * DT, (head + 1) * DT)
        total = None
        for index, piece in enumerate(pieces):
            places = lax.broadcasted_iota(jnp.int32, (DT, piece.shape[0]), 1)
            picked = jnp.where(channels[rows, :] - bases[index] == places, 1.0, 0.0).astype(jnp.bfloat16)
            part = jnp.dot(picked, piece[...], preferred_element_type=jnp.float32)
            total = part if total is None else total + part
        out[rows, :] = total.astype(jnp.bfloat16)


def choose(bases, channels, pieces, after):
    size = channels.shape[0]
    return pl.pallas_call(
        choose_kernel,
        out_shape=jax.ShapeDtypeStruct((size, ROWS), jnp.bfloat16),
        in_specs=[pl.BlockSpec(memory_space=pltpu.SMEM)]
        + [pl.BlockSpec(memory_space=pltpu.VMEM)] * 9
        + [pl.BlockSpec(memory_space=pl.ANY)] * len(after),
        out_specs=pl.BlockSpec(memory_space=pltpu.VMEM),
        compiler_params=pltpu.CompilerParams(vmem_limit_bytes=VMEM),
        cost_estimate=pl.CostEstimate(flops=2 * size * ROWS * TQ, bytes_accessed=3 << 20, transcendentals=0),
        name="choose",
    )(bases, channels, *pieces, *after)


def project_kernel(order, hidden, *refs):
    weights, outs, (wide, tall) = refs[:8], refs[-10:-2], refs[-2:]
    zh = order[8]
    for piece in range(8):
        columns = slice(piece * ROWS, (piece + 1) * ROWS)
        for place, head in enumerate((1 - zh, 2, zh)):
            rows = pl.ds(pl.multiple_of(head * DT, 16), DT)
            wide[place * DT : (place + 1) * DT, columns] = weights[piece][rows, :]
    for block in (2, 1, 3, 0):
        for piece in range(8):
            tall[:, piece * ROWS : (piece + 1) * ROWS] = hidden[order[piece], block * ROWS : (block + 1) * ROWS, :]
        for out, rows in ((outs[block], slice(0, 2 * DT)), (outs[4 + block], slice(2 * DT, 3 * DT))):
            out[...] = lax.dot_general(
                wide[rows, :], tall[...], (((1,), (1,)), ((), ())), preferred_element_type=jnp.float32
            )


def project(order, hidden, weights):
    sizes = [2 * DT] * 4 + [DT] * 4
    outs = pl.pallas_call(
        project_kernel,
        out_shape=[jax.ShapeDtypeStruct((size, ROWS), jnp.float32) for size in sizes],
        in_specs=[pl.BlockSpec(memory_space=pltpu.SMEM)]
        + [pl.BlockSpec(memory_space=pltpu.VMEM)] * 9,
        out_specs=[pl.BlockSpec(memory_space=pltpu.VMEM)] * 8,
        scratch_shapes=[pltpu.VMEM((3 * DT, 8 * ROWS), jnp.bfloat16), pltpu.VMEM((ROWS, 8 * ROWS), jnp.bfloat16)],
        compiler_params=pltpu.CompilerParams(vmem_limit_bytes=VMEM),
        cost_estimate=pl.CostEstimate(
            flops=24 * DT * ROWS * 8 * ROWS, bytes_accessed=(8 << 20) + 48 * DT * ROWS, transcendentals=0
        ),
        name="project",
    )(order, hidden, *weights)
    return outs[:4], outs[4:]


def add_parts(parts):
    moved = [lax.ppermute(parts[step], "y", back(step)) for step in (1, 2, 3)]
    return ((parts[0] + moved[0]) + (moved[1] + moved[2])).astype(jnp.bfloat16)


def join(mine, theirs, partners, student):
    return jnp.stack(
        [
            jnp.concatenate([mine, theirs[DT:], student[0]], axis=0),
            jnp.concatenate([partners, student[1]], axis=0),
        ]
    )


def fill_units(vectors, units):
    tch, tok, sch, sok = units
    zero = jnp.zeros((), jnp.bfloat16)
    t_pad = jnp.where(lax.broadcasted_iota(jnp.int32, (256 - DT, ROWS), 0) == 0, 1.0, 0.0).astype(jnp.bfloat16)
    s_pad = jnp.where(lax.broadcasted_iota(jnp.int32, (128 - DS, ROWS), 0) == 0, 1.0, 0.0).astype(jnp.bfloat16)
    for slot in range(SLOTS):
        for sub in range(2):
            for head in range(2):
                unit = (slot * 2 + sub) * 2 + head
                t = vectors[slot][sub, head * DT : (head + 1) * DT, :]
                s = vectors[slot][sub, 2 * DT + head * DS : 2 * DT + (head + 1) * DS, :]
                tch[unit, :DT, :] = t
                tch[unit, DT:, :] = t_pad
                sch[unit, :DS, :] = s
                sch[unit, DS:, :] = s_pad
                tok[unit] = jnp.concatenate([t, jnp.zeros((256 - DT, ROWS), jnp.bfloat16)], axis=0).T
                sok[unit] = jnp.concatenate([s, jnp.zeros((128 - DS, ROWS), jnp.bfloat16)], axis=0).T
    tch[NO_UNIT] = jnp.full((256, ROWS), zero)
    sch[NO_UNIT] = jnp.full((128, ROWS), zero)
    t_column = lax.broadcasted_iota(jnp.int32, (ROWS, 256), 1) == DT
    s_column = lax.broadcasted_iota(jnp.int32, (ROWS, 128), 1) == DS
    tok[NO_UNIT] = jnp.where(t_column, LOWEST, 0.0).astype(jnp.bfloat16)
    sok[NO_UNIT] = jnp.where(s_column, LOWEST, 0.0).astype(jnp.bfloat16)


def score(units, query, key):
    tch, tok, sch, sok = units
    return (
        jnp.dot(tok[key], tch[query], preferred_element_type=jnp.float32),
        jnp.dot(sok[key], sch[query], preferred_element_type=jnp.float32),
    )


def diagonal_scores(units, unit):
    t, s = score(units, unit, unit)
    visible = lax.broadcasted_iota(jnp.int32, (ROWS, ROWS), 0) <= lax.broadcasted_iota(jnp.int32, (ROWS, ROWS), 1)
    t = jnp.where(visible, t * (TEACHER_SCALE * LOG2E), LOWEST)
    return t, jnp.where(visible, s * (STUDENT_SCALE * LOG2E), LOWEST)


def walk(tasks, units, buffers, use):
    pairs = tasks[0]

    def load(task, buffer):
        query = tasks[1 + 3 * task]
        for half in range(2):
            t, s = score(units, query, tasks[2 + half + 3 * task])
            buffer[0, half * ROWS : (half + 1) * ROWS, :] = t * (TEACHER_SCALE * LOG2E)
            buffer[1, half * ROWS : (half + 1) * ROWS, :] = s * (STUDENT_SCALE * LOG2E)

    def take(task, buffer):
        use(tasks[1 + 3 * task], (tasks[2 + 3 * task], tasks[3 + 3 * task]), buffer)

    load(0, buffers[0])

    def two(pair, carry):
        load(2 * pair + 1, buffers[1])
        take(2 * pair, buffers[0])
        load(jnp.minimum(2 * pair + 2, 2 * pairs - 1), buffers[0])
        take(2 * pair + 1, buffers[1])
        return carry

    lax.fori_loop(0, pairs, two, 0)


def add_scores(stats, query, scores):
    old = stats[query]
    parts = [slice(start, start + CHUNK) for start in range(0, scores.shape[1], CHUNK)]

    def fold(values, combine):
        return combine(values.reshape(CHUNK // 8, 8, ROWS), axis=0)

    t_peak = s_peak = jnp.full((8, ROWS), LOWEST, jnp.float32)
    for part in parts:
        t_peak = jnp.maximum(t_peak, fold(scores[0, part, :], jnp.max))
        s_peak = jnp.maximum(s_peak, fold(scores[1, part, :], jnp.max))
    t_peak = jnp.maximum(jnp.max(t_peak, axis=0, keepdims=True), old[0:1])
    s_peak = jnp.maximum(jnp.max(s_peak, axis=0, keepdims=True), old[1:2])
    t_mass = s_mass = weighted = jnp.zeros((8, ROWS), jnp.float32)
    for part in parts:
        t, s = scores[0, part, :], scores[1, part, :]
        t_terms = jnp.exp2(t - t_peak)
        t_mass = t_mass + fold(t_terms, jnp.sum)
        weighted = weighted + fold(t_terms * (t - s), jnp.sum)
        s_mass = s_mass + fold(jnp.exp2(s - s_peak), jnp.sum)
    t_decay = jnp.exp2(old[0:1] - t_peak)
    s_decay = jnp.exp2(old[1:2] - s_peak)
    stats[query, 0:1, :] = t_peak
    stats[query, 1:2, :] = s_peak
    stats[query, 2:3, :] = old[2:3] * t_decay + jnp.sum(t_mass, axis=0, keepdims=True)
    stats[query, 3:4, :] = old[3:4] * s_decay + jnp.sum(s_mass, axis=0, keepdims=True)
    stats[query, 4:5, :] = old[4:5] * t_decay + jnp.sum(weighted, axis=0, keepdims=True)


DIAGONAL = (0, 2, 1)
ROW_UNITS = (0, 1)
COLUMN_UNITS = (2, 1)


def stats_kernel(tasks, *refs):
    vectors = [refs[OPERANDS.index(slot)] for slot in range(SLOTS)]
    along_row, along_column = refs[SLOTS : SLOTS + 2]
    units, stats, buffers = refs[SLOTS + 2 : SLOTS + 6], refs[SLOTS + 6], refs[SLOTS + 7 :]
    fill_units(vectors, units)
    for unit in range(UNITS + 1):
        stats[unit, 0:2, :] = jnp.full((2, ROWS), LOWEST, jnp.float32)
        stats[unit, 2:8, :] = jnp.zeros((6, ROWS), jnp.float32)
    for unit in DIAGONAL:
        block = buffers[0].at[:, :ROWS, :]
        block[0], block[1] = diagonal_scores(units, unit)
        add_scores(stats, unit, block)
    walk(tasks, units, buffers, lambda query, keys, buffer: add_scores(stats, query, buffer))
    for step in range(4):
        for out, slot, chosen in (
            (along_row, step, ROW_UNITS),
            (along_column, 3 + step if step else 0, COLUMN_UNITS),
        ):
            for place, unit in enumerate(chosen):
                first = (step * 2 + place) * 8
                out[first : first + 8, :] = stats[slot * 4 + unit]


UNIT_ARRAYS = [
    ((UNITS + 1, 256, ROWS), jnp.bfloat16),
    ((UNITS + 1, ROWS, 256), jnp.bfloat16),
    ((UNITS + 1, 128, ROWS), jnp.bfloat16),
    ((UNITS + 1, ROWS, 128), jnp.bfloat16),
]
BUFFERS = [((2, 2 * ROWS, ROWS), jnp.float32)] * 2


def row_stats(tasks, vectors):
    scratch = [((UNITS + 1, 8, ROWS), jnp.float32)] + BUFFERS
    along_row, along_column, *units = pl.pallas_call(
        stats_kernel,
        out_shape=[jax.ShapeDtypeStruct((64, ROWS), jnp.float32)] * 2
        + [jax.ShapeDtypeStruct(s, d) for s, d in UNIT_ARRAYS],
        in_specs=[pl.BlockSpec(memory_space=pltpu.SMEM)] + [pl.BlockSpec(memory_space=pltpu.VMEM)] * SLOTS,
        out_specs=[pl.BlockSpec(memory_space=pltpu.VMEM)] * 6,
        scratch_shapes=[pltpu.VMEM(s, d) for s, d in scratch],
        compiler_params=pltpu.CompilerParams(vmem_limit_bytes=VMEM),
        name="row_stats",
    )(tasks, *[vectors[slot] for slot in OPERANDS])
    return along_row, along_column, units


def merge_rows(parts):
    t_peak, s_peak = parts[0][0:1], parts[0][1:2]
    for part in parts[1:]:
        t_peak = jnp.maximum(t_peak, part[0:1])
        s_peak = jnp.maximum(s_peak, part[1:2])
    t_mass = s_mass = weighted = jnp.zeros((1, ROWS), jnp.float32)
    for part in parts:
        t_decay = jnp.exp2(part[0:1] - t_peak)
        t_mass = t_mass + part[2:3] * t_decay
        s_mass = s_mass + part[3:4] * jnp.exp2(part[1:2] - s_peak)
        weighted = weighted + part[4:5] * t_decay
    t_total = t_peak + jnp.log(t_mass) * LOG2E
    s_total = s_peak + jnp.log(s_mass) * LOG2E
    return t_total, s_total, (weighted / t_mass - t_total + s_total) * LN2


def merge_parts(rows, columns, total, divergence):
    def of(line, step, place):
        entries = [((step - ahead) % 4 * 2 + place) * 8 for ahead in range(4)]
        return [part[entry : entry + 8, :] for part, entry in zip(line, entries)]

    divergence[...] = jnp.zeros((8, ROWS), jnp.float32)
    cases = [(0, 0, of(rows, 0, 0)), (0, 2, of(columns, 0, 0)), (0, 1, of(rows, 0, 1) + of(columns, 0, 1)[1:])]
    for step in (1, 2, 3):
        cases += [(step, unit, of(rows, step, place)) for place, unit in enumerate(ROW_UNITS)]
        cases += [(3 + step, unit, of(columns, step, place)) for place, unit in enumerate(COLUMN_UNITS)]
    for index, (slot, unit, parts) in enumerate(cases):
        t_total, s_total, value = merge_rows(parts)
        total[slot * 4 + unit, 0:1, :] = t_total - LOG2_SCALE
        total[slot * 4 + unit, 1:2, :] = s_total - LOG2_SCALE
        if index < 3:
            divergence[index : index + 1, :] = value


def grad_kernel(tasks, *refs):
    units, refs = refs[:4], refs[4:]
    rows, columns, outs, divergence = refs[:4], refs[4:8], refs[8 : 8 + SLOTS], refs[8 + SLOTS]
    rest = refs[9 + SLOTS :]
    total, grad, buffers = rest[0], rest[1], rest[2:]
    sch = units[2]
    merge_parts(rows, columns, total, divergence)
    total[NO_UNIT] = jnp.full((8, ROWS), -LOWEST, jnp.float32)
    grad[...] = jnp.zeros((UNITS + 1, DS, ROWS), jnp.float32)

    def add(query, key, t, s):
        t_prob = jnp.exp2(t - total[query, 0:1, :])
        s_prob = jnp.exp2(s - total[query, 1:2, :])
        weights = (s_prob - t_prob).astype(jnp.bfloat16)
        grad[query] += jnp.dot(sch[key, :DS, :], weights, preferred_element_type=jnp.float32)
        grad[key] += lax.dot_general(
            sch[query, :DS, :], weights, (((1,), (1,)), ((), ())), preferred_element_type=jnp.float32
        )

    def use(query, keys, buffer):
        for half in range(2):
            part = slice(half * ROWS, (half + 1) * ROWS)
            add(query, keys[half], buffer[0, part, :], buffer[1, part, :])

    for unit in DIAGONAL:
        add(unit, unit, *diagonal_scores(units, unit))
    walk(tasks, units, buffers, use)
    for slot in range(SLOTS):
        for unit in range(4):
            outs[slot][unit * DS : (unit + 1) * DS, :] = grad[slot * 4 + unit]


def gradients(tasks, units, rows, columns):
    scratch = [((UNITS + 1, 8, ROWS), jnp.float32), ((UNITS + 1, DS, ROWS), jnp.float32)] + BUFFERS
    outs = pl.pallas_call(
        grad_kernel,
        out_shape=[jax.ShapeDtypeStruct((4 * DS, ROWS), jnp.float32)] * SLOTS
        + [jax.ShapeDtypeStruct((8, ROWS), jnp.float32)],
        in_specs=[pl.BlockSpec(memory_space=pltpu.SMEM)] + [pl.BlockSpec(memory_space=pltpu.VMEM)] * 12,
        out_specs=[pl.BlockSpec(memory_space=pltpu.VMEM)] * (SLOTS + 1),
        scratch_shapes=[pltpu.VMEM(s, d) for s, d in scratch],
        compiler_params=pltpu.CompilerParams(vmem_limit_bytes=VMEM),
        name="gradients",
    )(tasks, *units, *rows, *columns)
    return outs[:SLOTS], outs[SLOTS]


def to_line(block, axis):
    return [block] + [lax.ppermute(block, axis, back(step)) for step in (1, 2, 3)]


def pair_students(student, zh):
    heads = student.reshape(3, DS, ROWS)
    mine = jnp.concatenate([jnp.where(zh == 0, heads[0], heads[1]), heads[2]], axis=0)
    theirs = jnp.concatenate([jnp.where(zh == 0, heads[1], heads[0]), heads[2]], axis=0)
    return jnp.stack([mine, lax.ppermute(theirs, "zh", SWAP)])


def shards(hidden, q_weight, regroup, student_rel):
    x, zh, y = lax.axis_index("x"), lax.axis_index("zh"), lax.axis_index("y")
    head = lax.axis_index(HEAD)
    place = x * 8 + zh * 4 + y
    tasks = lax.dynamic_index_in_dim(jnp.asarray(plan()), place, 0, keepdims=False)

    zl, core = lax.axis_index("zl"), lax.axis_index("core")
    line = to_line(q_weight.T, "zl")
    columns = line + [lax.ppermute(piece, "core", SWAP) for piece in line]
    owners = (zl + jnp.arange(4, dtype=jnp.int32)) % 4 * 2
    bases = jnp.concatenate([owners + core, owners + 1 - core]) * columns[0].shape[0]

    quarters = [lax.dynamic_slice(hidden, (0, (y + step) % 4 * ROWS), (ROWS, ROWS)) for step in range(4)]
    quarters = quarters[:1] + [lax.ppermute(quarters[step], "y", forth(step)) for step in (1, 2, 3)]
    quarters[0] = hold(quarters[0], line[1])
    features = lax.all_gather(jnp.concatenate(quarters, axis=0), HEAD, axis=0)

    pair = pair_students(student_rel.T, zh)
    channels = lax.dynamic_slice_in_dim(regroup, head * (3 * DT), 3 * DT, 0)
    chosen = choose(bases, channels[:, None], columns, (pair,))
    other = lax.ppermute(chosen, "zh", SWAP)
    pieces = to_line(chosen, "x") + to_line(other, "x")
    around = (x + jnp.arange(4, dtype=jnp.int32)) % 4 * 2
    order = jnp.concatenate([around + zh, around + 1 - zh, zh.reshape(1)])

    theirs, mine = project(order, features, pieces)
    theirs = add_parts(theirs)
    partners = lax.ppermute(theirs, "zh", SWAP)
    vectors = to_slots(join(add_parts(mine), theirs, partners, pair))

    along_row, along_column, units = row_stats(tasks, vectors)
    grads, divergence = gradients(tasks, units, to_line(along_row, "y"), to_line(along_column, "x"))
    grads = to_owners(grads)
    grad = grads[0]
    for piece in grads[1:]:
        grad = grad + piece

    swapped = lax.ppermute(jnp.concatenate([grad[2 * DS :], divergence], axis=0), "zh", SWAP)
    first = jnp.where(zh == 0, grad[:DS], swapped[:DS])
    second = jnp.where(zh == 0, swapped[:DS], grad[:DS])
    third = grad[DS : 2 * DS] + swapped[DS : 2 * DS]
    student_grad = jnp.concatenate([first, second, third], axis=0).T

    away = swapped[2 * DS + 1]
    first = jnp.where(zh == 0, divergence[0], away)
    second = jnp.where(zh == 0, away, divergence[0])
    return student_grad, jnp.stack([first, second, divergence[2]], axis=1)


def solution(mesh):
    whole = Mesh(mesh.devices.reshape(4, 2, 4, 4, 2), CTX + HEAD)
    split = P(CTX, HEAD)
    return jax.shard_map(
        shards,
        mesh=whole,
        in_specs=(split, split, P(), split),
        out_specs=(split, split),
        check_vma=False,
    )
```
